32 devices in a mesh: cell: 4 (over z), level: 4 (over y, x), rep: 2 (over core).
Axes of the slice: x: 2, y: 2, z: 4, core: 2. Of those that a mesh axis runs over, the one named last changes fastest.
Arguments:
- resident_pos: float32 [2, 32, 128, 512], P(None, 'rep', 'level', 'cell'), may hold values from -0.5 to 0.5
- resident_strength: float32 [32, 128, 512], P('rep', 'level', 'cell'), may hold values from -0.51 to 0.51
- mover_pos: float32 [2, 2, 4, 16384], P(None, 'rep', 'level', 'cell'), may hold values from -0.5 to 0.5
- mover_strength: float32 [2, 4, 16384], P('rep', 'level', 'cell'), may hold values from -0.51 to 0.51
- mover_owner: int32 [2, 4, 16384], P('rep', 'level', 'cell'), may hold values from 0 to 3, as said below
- mover_leaf: int32 [2, 4, 16384], P('rep', 'level', 'cell'), may hold values from 0 to 4095, as said below
- mover_slot: int32 [2, 4, 16384], P('rep', 'level', 'cell'), may hold values from 0 to 15
Outputs:
- velocity: float32 [2, 32, 128, 512], P(None, 'rep', 'level', 'cell')
The draws below stay inside these ranges and needn't reach their ends.
Inputs may be any that keep to these rules, and one draw needn't show every extreme that they name: `mover_owner`: for one rep and level index, the 4096 movers of one device name one owner at most 1024 times, and one owner is named exactly 1024 times by every device. `mover_leaf`: leaf key y * 128 + x inside the owner's domain; for one rep and level index no (owner, leaf, slot) triple appears twice.
All inputs are finite; a program needn't handle non-finite values.
Results may differ from the reference program's by a relative error of at most 0.0003.
Values sent between devices are 32-bit elements; how exact they have to be, the bound alone decides.
A program may use at most 192 MiB of HBM per device.

```python
import math
import jax
import jax.numpy as jnp
import numpy as np
from jax import lax

ORDER = 10
SLOT = 32
MOVE = 4096
SY = 32
SX = 128
HALF = 16
CAP = 1024
N_CELL = 4
N_LEVEL = 4
N_REP = 2


centre_weight = -5.0 / 3.0


def mover_routes(key):
    cell_count = N_CELL
    owned_slots = HALF * SX * SY
    leaves = SX * SY
    row_keys = jax.random.split(key, N_REP * N_LEVEL)

    def one_row(row_key):
        busy_key, pick_key, place_key = jax.random.split(row_key, 3)
        busiest = jax.random.randint(busy_key, (), 0, cell_count).astype(jnp.int32)
        others = (busiest + 1 + jnp.arange(cell_count - 1, dtype=jnp.int32)) % cell_count
        candidate = jnp.repeat(others, CAP)

        def one_source(source_key):
            pick_first, pick_second = jax.random.split(source_key)
            chosen = jax.random.permutation(pick_first, candidate)[:3 * CAP]
            named = jnp.concatenate([jnp.full((CAP,), busiest, jnp.int32), chosen.astype(jnp.int32)])
            return jax.random.permutation(pick_second, named)
        owners = jax.vmap(one_source)(jax.random.split(pick_key, cell_count))
        flat_owner = owners.reshape(-1)
        sort_order = jnp.argsort(flat_owner, stable=True)
        sorted_owner = flat_owner[sort_order]
        starts = jnp.searchsorted(sorted_owner, jnp.arange(cell_count, dtype=jnp.int32)).astype(jnp.int32)
        sorted_rank = jnp.arange(flat_owner.shape[0], dtype=jnp.int32) - starts[sorted_owner]
        rank_in_owner = jnp.zeros_like(flat_owner).at[sort_order].set(sorted_rank)

        def one_owner(owner_key):
            remaining = jax.random.permutation(owner_key, owned_slots - 2).astype(jnp.int32) + 1
            return jnp.concatenate([jnp.array([owned_slots - 1, 0], jnp.int32), remaining])
        places = jax.vmap(one_owner)(jax.random.split(place_key, cell_count))
        chosen_place = places[flat_owner, rank_in_owner]
        return (flat_owner, chosen_place % leaves, chosen_place // leaves)
    owners, leaf_keys, slot_keys = jax.vmap(one_row)(row_keys)
    out_shape = (N_REP, N_LEVEL, N_CELL * MOVE)
    return (owners.reshape(out_shape), leaf_keys.reshape(out_shape), slot_keys.reshape(out_shape))


def draw_mover_owner(key, part):
    return mover_routes(key)[0]


def draw_mover_leaf(key, part):
    return mover_routes(key)[1]


def draw_mover_slot(key, part):
    return mover_routes(key)[2]


def resident_corners(key):
    return jax.random.bernoulli(jax.random.fold_in(key, 101), 0.625, (SLOT, SY * N_LEVEL, SX * N_CELL))


def mover_corners(key):
    return jax.random.bernoulli(jax.random.fold_in(key, 102), 0.625, (N_REP, N_LEVEL, N_CELL * MOVE))


def corner_offsets(side_key, corners, jitter, centre):
    sides = jnp.where(jax.random.bernoulli(side_key, 0.5, jitter.shape), 1.0, -1.0)
    at_corner = sides * (0.5 - jitter)
    return jnp.where(corners[None], at_corner, centre).astype(jnp.float32)


def draw_resident_pos(key, part):
    corners = resident_corners(key)
    key = jax.random.fold_in(key, 23)
    side_key, jitter_key, centre_key = jax.random.split(key, 3)
    out_shape = (2,) + corners.shape
    jitter = jax.random.uniform(jitter_key, out_shape, jnp.float32, 0.0, 0.01)
    centre = jnp.clip(0.04 * jax.random.normal(centre_key, out_shape, jnp.float32), -0.1, 0.1)
    return corner_offsets(side_key, corners, jitter, centre)


def draw_mover_pos(key, part):
    corners = mover_corners(key)
    key = jax.random.fold_in(key, 24)
    side_key, jitter_key, centre_key = jax.random.split(key, 3)
    out_shape = (2,) + corners.shape
    jitter = jax.random.uniform(jitter_key, out_shape, jnp.float32, 0.0, 0.01)
    centre = jnp.clip(0.04 * jax.random.normal(centre_key, out_shape, jnp.float32), -0.1, 0.1)
    return corner_offsets(side_key, corners, jitter, centre)


def draw_resident_strength(key, part):
    corners = resident_corners(key)
    key = jax.random.fold_in(key, 21)
    sign_key, size_key = jax.random.split(key)
    out_shape = corners.shape
    leaf_sign = jnp.where(jax.random.bernoulli(sign_key, 0.5, out_shape[1:]), 1.0, -1.0)[None]
    weight = jnp.where(corners, 1.0, centre_weight)
    sizes = jnp.exp(jax.random.uniform(size_key, out_shape, jnp.float32, math.log(0.15), math.log(0.3)))
    return (leaf_sign * sizes * weight).astype(jnp.float32)


def draw_mover_strength(key, part):
    corners = mover_corners(key)
    key = jax.random.fold_in(key, 22)
    sign_key, size_key = jax.random.split(key)
    out_shape = corners.shape
    signs = jnp.where(jax.random.bernoulli(sign_key, 0.5, out_shape), 1.0, -1.0)
    weight = jnp.where(corners, 1.0, centre_weight)
    sizes = jnp.exp(jax.random.uniform(size_key, out_shape, jnp.float32, math.log(0.15), math.log(0.3)))
    return (signs * sizes * weight).astype(jnp.float32)


def setup_inputs(seed: int = 0) -> dict:
    splits = jax.random.split(jax.random.key(seed), 8)
    return {
        "resident_pos": draw_resident_pos(jax.random.fold_in(splits[7], 71), 0),
        "resident_strength": draw_resident_strength(jax.random.fold_in(splits[7], 71), 0),
        "mover_pos": draw_mover_pos(jax.random.fold_in(splits[7], 71), 0),
        "mover_strength": draw_mover_strength(jax.random.fold_in(splits[7], 71), 0),
        "mover_owner": draw_mover_owner(jax.random.fold_in(splits[7], 71), 0),
        "mover_leaf": draw_mover_leaf(jax.random.fold_in(splits[7], 71), 0),
        "mover_slot": draw_mover_slot(jax.random.fold_in(splits[7], 71), 0),
    }


precise = lax.Precision.HIGHEST
blob_square = 0.09


def real_form(matrix):
    top_rows = np.concatenate([matrix.real, -matrix.imag], axis=1)
    low_rows = np.concatenate([matrix.imag, matrix.real], axis=1)
    return np.concatenate([top_rows, low_rows], axis=0)


def child_offset(parity_x, parity_y):
    return complex((parity_x - 0.5) / 2.0, (parity_y - 0.5) / 2.0)


def upward_table(parity_x, parity_y):
    offset = child_offset(parity_x, parity_y)
    matrix = np.zeros((ORDER, ORDER), complex)
    for k in range(ORDER):
        for m in range(k + 1):
            matrix[k, m] = math.comb(k, m) * 0.5 ** m * offset ** (k - m)
    return real_form(matrix)


def downward_table(parity_x, parity_y):
    offset = child_offset(parity_x, parity_y)
    matrix = np.zeros((ORDER, ORDER), complex)
    for m in range(ORDER):
        for l in range(m, ORDER):
            matrix[m, l] = 0.5 ** (m + 1) * math.comb(l, m) * offset ** (l - m)
    return real_form(matrix)


def far_table(step_x, step_y):
    distance = complex(step_x, step_y)
    matrix = np.zeros((ORDER, ORDER), complex)
    for l in range(ORDER):
        for k in range(ORDER):
            matrix[l, k] = (-1) ** (k + 1) * math.comb(k + l, l) * distance ** (-(k + l + 1))
    return real_form(matrix)


def apply_matrix(matrix, level_field):
    return jnp.einsum("ij,jyx->iyx", jnp.asarray(matrix, dtype=jnp.float32), level_field, precision=precise)


def upward(level_field):
    summed = None
    for parity_y in (0, 1):
        for parity_x in (0, 1):
            product = apply_matrix(upward_table(parity_x, parity_y), level_field[:, parity_y::2, parity_x::2])
            summed = product if summed is None else summed + product
    return summed


def downward(parent):
    channels, cells_y, cells_x = parent.shape
    pieces = jnp.stack([jnp.stack([apply_matrix(downward_table(parity_x, parity_y), parent) for parity_x in (0, 1)]) for parity_y in (0, 1)])
    return pieces.transpose(2, 3, 0, 4, 1).reshape(channels, 2 * cells_y, 2 * cells_x)


def interactions(level_field, at_top):
    channels, cells_y, cells_x = level_field.shape
    reach_y = cells_y - 1 if at_top else 3
    reach_x = cells_x - 1 if at_top else 3
    padded = jnp.pad(level_field, ((0, 0), (reach_y, reach_y), (reach_x, reach_x)))
    parity_y = (jnp.arange(cells_y, dtype=jnp.int32) % 2)[:, None]
    parity_x = (jnp.arange(cells_x, dtype=jnp.int32) % 2)[None, :]
    summed = jnp.zeros(level_field.shape, jnp.float32)
    for step_y in range(-reach_y, reach_y + 1):
        for step_x in range(-reach_x, reach_x + 1):
            if max(abs(step_x), abs(step_y)) <= 1:
                continue
            source = padded[:, reach_y + step_y:reach_y + step_y + cells_y, reach_x + step_x:reach_x + step_x + cells_x]
            product = apply_matrix(far_table(step_x, step_y), source)
            if not at_top:
                inside = (parity_x + step_x >= -2) & (parity_x + step_x <= 3) & (parity_y + step_y >= -2) & (parity_y + step_y <= 3)
                product = product * inside.astype(jnp.float32)[None]
            summed = summed + product
    return summed


def moments(pos_x, pos_y, strength):
    real_power = jnp.ones_like(pos_x)
    imag_power = jnp.zeros_like(pos_x)
    real_rows = []
    imag_rows = []
    for k in range(ORDER):
        real_rows.append(jnp.sum(strength * real_power, axis=0))
        imag_rows.append(jnp.sum(strength * imag_power, axis=0))
        real_power, imag_power = real_power * pos_x - imag_power * pos_y, real_power * pos_y + imag_power * pos_x
    return jnp.stack(real_rows + imag_rows)


def evaluate(local_field, pos_x, pos_y):
    real_acc = jnp.broadcast_to(local_field[ORDER - 1], pos_x.shape)
    imag_acc = jnp.broadcast_to(local_field[2 * ORDER - 1], pos_x.shape)
    for l in range(ORDER - 2, -1, -1):
        real_acc, imag_acc = (real_acc * pos_x - imag_acc * pos_y + local_field[l],
                              real_acc * pos_y + imag_acc * pos_x + local_field[ORDER + l])
    return real_acc, imag_acc


def near_field(particles):
    slot_count, cells_y, cells_x = particles.shape[1:]
    padded = jnp.pad(particles, ((0, 0), (0, 0), (1, 1), (1, 1)))
    band_rows = 8
    keep_mask = (1.0 - jnp.eye(slot_count, dtype=jnp.float32))[:, :, None, None]

    def one_band(row_start):
        target = lax.dynamic_slice_in_dim(particles, row_start, band_rows, 2)
        real_sum = jnp.zeros((slot_count, band_rows, cells_x), jnp.float32)
        imag_sum = jnp.zeros((slot_count, band_rows, cells_x), jnp.float32)
        for step_y in (-1, 0, 1):
            row_band = lax.dynamic_slice_in_dim(padded, row_start + 1 + step_y, band_rows, 2)
            for step_x in (-1, 0, 1):
                source = row_band[:, :, :, 1 + step_x:1 + step_x + cells_x]
                gap_x = target[0][:, None] - source[0][None] - step_x
                gap_y = target[1][:, None] - source[1][None] - step_y
                weight = source[2][None] / (gap_x * gap_x + gap_y * gap_y + blob_square)
                if step_x == 0 and step_y == 0:
                    weight = weight * keep_mask
                real_sum = real_sum + jnp.sum(weight * gap_x, axis=1)
                imag_sum = imag_sum - jnp.sum(weight * gap_y, axis=1)
        return jnp.stack([real_sum, imag_sum])

    starts = jnp.arange(0, cells_y, band_rows, dtype=jnp.int32)
    bands = lax.map(one_band, starts)
    return bands.transpose(1, 2, 0, 3, 4).reshape(2, slot_count, cells_y, cells_x)


def reference(resident_pos, resident_strength, mover_pos, mover_strength, mover_owner, mover_leaf, mover_slot):
    wide_x = SX * N_CELL
    wide_y = SY * N_LEVEL
    rep_index = jnp.arange(N_REP, dtype=jnp.int32)[:, None, None]
    level_index = jnp.arange(N_LEVEL, dtype=jnp.int32)[None, :, None]
    slot_index = rep_index * HALF + mover_slot
    row_index = level_index * SY + mover_leaf // SX
    column_index = mover_owner * SX + mover_leaf % SX
    flat_index = ((slot_index * wide_y + row_index) * wide_x + column_index).reshape(-1)
    resident = jnp.concatenate([resident_pos.reshape(2, -1), resident_strength.reshape(1, -1)])
    incoming = jnp.concatenate([mover_pos.reshape(2, -1), mover_strength.reshape(1, -1)])
    particles = resident.at[:, flat_index].set(incoming).reshape(3, SLOT, wide_y, wide_x)
    level_fields = [moments(particles[0], particles[1], particles[2])]
    top_level = min(wide_x, wide_y).bit_length() - 1
    for k in range(top_level):
        level_fields.append(upward(level_fields[-1]))
    local_field = interactions(level_fields[top_level], True)
    for k in range(top_level - 1, -1, -1):
        local_field = interactions(level_fields[k], False) + downward(local_field)
    far_real, far_imag = evaluate(local_field, particles[0], particles[1])
    near = near_field(particles)
    real_part = near[0] + far_real
    imag_part = near[1] + far_imag
    return jnp.stack([imag_part, real_part]) / (2.0 * math.pi)
```

```python
import math

import jax
import jax.numpy as jnp
import numpy as np
from jax import lax
from jax.experimental import pallas as pl
from jax.experimental.pallas import tpu as pltpu
from jax.sharding import PartitionSpec as P

ORDER = 10
HALO_LEVELS = 4
CAP = 1024


precise = lax.Precision.HIGHEST
blob_square = 0.09


def with_halo(shard, sides, width):
    for axis, dim in sides:
        devices, length = (lax.axis_size(axis), shard.shape[dim])
        up = [(i, (i + 1) % devices) for i in range(devices - 1)]
        down = [(j, i) for i, j in up]
        last = lax.slice_in_dim(shard, length - width, length, axis=dim)
        first = lax.slice_in_dim(shard, 0, width, axis=dim)
        before = lax.ppermute(last, axis, up)
        after = lax.ppermute(first, axis, down)
        shard = jnp.concatenate([before, shard, after], axis=dim)
    return shard


def real_form(matrix):
    top_rows = np.concatenate([matrix.real, -matrix.imag], axis=1)
    low_rows = np.concatenate([matrix.imag, matrix.real], axis=1)
    return np.concatenate([top_rows, low_rows], axis=0)


def child_offset(parity_x, parity_y):
    return complex((parity_x - 0.5) / 2.0, (parity_y - 0.5) / 2.0)


def upward_table(parity_x, parity_y):
    offset = child_offset(parity_x, parity_y)
    matrix = np.zeros((ORDER, ORDER), complex)
    for k in range(ORDER):
        for m in range(k + 1):
            matrix[k, m] = math.comb(k, m) * 0.5**m * offset ** (k - m)
    return real_form(matrix)


def downward_table(parity_x, parity_y):
    offset = child_offset(parity_x, parity_y)
    matrix = np.zeros((ORDER, ORDER), complex)
    for m in range(ORDER):
        for l in range(m, ORDER):
            matrix[m, l] = 0.5 ** (m + 1) * math.comb(l, m) * offset ** (l - m)
    return real_form(matrix)


def far_table(step_x, step_y):
    distance = complex(step_x, step_y)
    matrix = np.zeros((ORDER, ORDER), complex)
    for l in range(ORDER):
        for k in range(ORDER):
            matrix[l, k] = (-1) ** (k + 1) * math.comb(k + l, l) * distance ** (-(k + l + 1))
    return real_form(matrix)


def apply_matrix(matrix, level_field):
    return jnp.einsum(
        "ij,jyx->iyx", jnp.asarray(matrix, dtype=jnp.float32), level_field, precision=precise
    )


def upward(level_field):
    summed = None
    for parity_y in (0, 1):
        for parity_x in (0, 1):
            product = apply_matrix(
                upward_table(parity_x, parity_y), level_field[:, parity_y::2, parity_x::2]
            )
            summed = product if summed is None else summed + product
    return summed


def downward(parent):
    channels, cells_y, cells_x = parent.shape
    pieces = jnp.stack(
        [
            jnp.stack(
                [apply_matrix(downward_table(parity_x, parity_y), parent) for parity_x in (0, 1)]
            )
            for parity_y in (0, 1)
        ]
    )
    return pieces.transpose(2, 3, 0, 4, 1).reshape(channels, 2 * cells_y, 2 * cells_x)


def grouped_far(padded, margin_cells, cells_y, cells_x):
    classes = []
    for parity_y in (0, 1):
        row_parts = []
        for parity_x in (0, 1):
            pieces = []
            blocks = []
            for step_y in range(-2 - parity_y, 4 - parity_y):
                for step_x in range(-2 - parity_x, 4 - parity_x):
                    if max(abs(step_x), abs(step_y)) <= 1:
                        continue
                    first_y = margin_cells + parity_y + step_y
                    first_x = margin_cells + parity_x + step_x
                    pieces.append(
                        padded[:, first_y : first_y + cells_y : 2, first_x : first_x + cells_x : 2]
                    )
                    blocks.append(far_table(step_x, step_y))
            row_parts.append(
                apply_matrix(np.concatenate(blocks, axis=1), jnp.concatenate(pieces, axis=0))
            )
        classes.append(jnp.stack(row_parts))
    joined = jnp.stack(classes)
    return joined.transpose(2, 3, 0, 4, 1).reshape(joined.shape[2], cells_y, cells_x)


def top_far(level_field):
    channels, cells_y, cells_x = level_field.shape
    reach_y = cells_y - 1
    reach_x = cells_x - 1
    padded = jnp.pad(level_field, ((0, 0), (reach_y, reach_y), (reach_x, reach_x)))
    summed = jnp.zeros(level_field.shape, jnp.float32)
    for step_y in range(-reach_y, reach_y + 1):
        for step_x in range(-reach_x, reach_x + 1):
            if max(abs(step_x), abs(step_y)) <= 1:
                continue
            source = padded[
                :,
                reach_y + step_y : reach_y + step_y + cells_y,
                reach_x + step_x : reach_x + step_x + cells_x,
            ]
            summed = summed + apply_matrix(far_table(step_x, step_y), source)
    return summed


def moments(pos_x, pos_y, strength):
    real_power = jnp.ones_like(pos_x)
    imag_power = jnp.zeros_like(pos_x)
    real_rows = []
    imag_rows = []
    for k in range(ORDER):
        real_rows.append(jnp.sum(strength * real_power, axis=0))
        imag_rows.append(jnp.sum(strength * imag_power, axis=0))
        real_power, imag_power = (
            real_power * pos_x - imag_power * pos_y,
            real_power * pos_y + imag_power * pos_x,
        )
    return jnp.stack(real_rows + imag_rows)


BAND = 8
GROUP = 8


def near_kernel(src_ref, own_ref, local_ref, out_ref):
    half_slots, cells_y, cells_x = own_ref.shape[1:]
    slot_count = src_ref.shape[2]
    scale = 1.0 / (2.0 * math.pi)

    def one_block(index, carry):
        row = pl.multiple_of((index // (half_slots // GROUP)) * BAND, BAND)
        slot = (index % (half_slots // GROUP)) * GROUP
        here = pl.ds(row, BAND)
        target_x = [own_ref[0, slot + t, here, :] for t in range(GROUP)]
        target_y = [own_ref[1, slot + t, here, :] for t in range(GROUP)]

        def one_source(s, sums):
            sums = list(sums)
            for step_y in (-1, 0, 1):
                there = pl.ds(row + 1 + step_y, BAND)
                for step_x in (-1, 0, 1):
                    source_x = src_ref[step_x + 1, 0, s, there, :] + float(step_x)
                    source_y = src_ref[step_x + 1, 1, s, there, :] + float(step_y)
                    strength = src_ref[step_x + 1, 2, s, there, :]
                    for t in range(GROUP):
                        gap_x = target_x[t] - source_x
                        gap_y = target_y[t] - source_y
                        square = gap_x * gap_x + (gap_y * gap_y + blob_square)
                        weight = strength * pl.reciprocal(square, approx=True)
                        sums[t] = sums[t] + weight * gap_x
                        sums[GROUP + t] = sums[GROUP + t] + weight * gap_y
            return tuple(sums)

        zero = jnp.zeros((BAND, cells_x), jnp.float32)
        sums = lax.fori_loop(0, slot_count, one_source, (zero,) * (2 * GROUP))
        for t in range(GROUP):
            real_acc = local_ref[ORDER - 1, here, :]
            imag_acc = local_ref[2 * ORDER - 1, here, :]
            for l in range(ORDER - 2, -1, -1):
                real_acc, imag_acc = (
                    real_acc * target_x[t] - imag_acc * target_y[t] + local_ref[l, here, :],
                    real_acc * target_y[t] + imag_acc * target_x[t] + local_ref[ORDER + l, here, :],
                )
            out_ref[0, slot + t, here, :] = (imag_acc - sums[GROUP + t]) * scale
            out_ref[1, slot + t, here, :] = (real_acc + sums[t]) * scale
        return carry

    lax.fori_loop(0, (cells_y // BAND) * (half_slots // GROUP), one_block, 0)


def near_and_far(shifted, own, local_field):
    vmem = pl.BlockSpec(memory_space=pltpu.VMEM)
    return pl.pallas_call(
        near_kernel,
        out_shape=jax.ShapeDtypeStruct((2,) + own.shape[1:], jnp.float32),
        in_specs=[vmem] * 3,
        out_specs=vmem,
        compiler_params=pltpu.CompilerParams(vmem_limit_bytes=48 * 1024 * 1024),
        name="near_and_far",
    )(shifted, own, local_field)


def framing(level_field):
    return with_halo(level_field, (("cell", 2), ("level", 1)), 3)


def local(
    resident_pos, resident_strength, mover_pos, mover_strength, mover_owner, mover_leaf, mover_slot
):
    cell_count = lax.axis_size("cell")
    level_count = lax.axis_size("level")
    half_slots, cells_y, cells_x = resident_strength.shape
    leaves = cells_y * cells_x
    owner_cell = mover_owner.reshape(-1)
    address = mover_slot.reshape(-1) * leaves + mover_leaf.reshape(-1)
    peer_ids = jnp.arange(cell_count, dtype=jnp.int32)
    onehot = (owner_cell[:, None] == peer_ids[None, :]).astype(jnp.int32)
    rank_in_owner = jnp.sum(jnp.cumsum(onehot, axis=0) * onehot, axis=1) - 1
    values = jnp.concatenate([mover_pos.reshape(2, -1), mover_strength.reshape(1, -1)])
    outgoing = (
        jnp.zeros((3, cell_count, CAP), jnp.float32).at[:, owner_cell, rank_in_owner].set(values)
    )
    addresses = (
        jnp.full((1, cell_count, CAP), half_slots * leaves, jnp.int32)
        .at[0, owner_cell, rank_in_owner]
        .set(address)
    )
    arrived, arrived_at = (
        lax.all_to_all(outgoing, "cell", split_axis=1, concat_axis=1, tiled=True),
        lax.all_to_all(addresses, "cell", split_axis=1, concat_axis=1, tiled=True),
    )
    resident = jnp.concatenate([resident_pos.reshape(2, -1), resident_strength.reshape(1, -1)])
    settled = resident.at[:, arrived_at.reshape(-1)].set(arrived.reshape(3, -1), mode="drop")
    particles = settled.reshape(3, half_slots, cells_y, cells_x)
    whole = lax.all_gather(particles, "rep", axis=1, tiled=True)
    framed = with_halo(whole, (("cell", 3), ("level", 2)), 1)
    whole_inner = framed[:, :, 1:-1, 1:-1]
    level_zero = moments(whole_inner[0], whole_inner[1], whole_inner[2])
    owned = [level_zero]
    for k in range(HALO_LEVELS):
        owned.append(upward(owned[-1]))
    framed_levels = [framing(owned[k]) for k in range(HALO_LEVELS)]
    coarse_own = owned[HALO_LEVELS]
    channels, coarse_y, coarse_x = coarse_own.shape
    collected = lax.all_gather(coarse_own[None], ("cell", "level"), axis=0, tiled=True)
    coarse_grid = collected.reshape(cell_count, level_count, channels, coarse_y, coarse_x)
    coarse_grid = coarse_grid.transpose(2, 1, 3, 0, 4).reshape(
        channels, level_count * coarse_y, cell_count * coarse_x
    )
    coarse_fields = [coarse_grid]
    top_level = min(cell_count * cells_x, level_count * cells_y).bit_length() - 1
    for k in range(HALO_LEVELS + 1, top_level + 1):
        coarse_fields.append(upward(coarse_fields[-1]))
    local_field = top_far(coarse_fields[-1])
    for index in range(len(coarse_fields) - 2, -1, -1):
        level_field = coarse_fields[index]
        padded = jnp.pad(level_field, ((0, 0), (3, 3), (3, 3)))
        local_field = grouped_far(padded, 3, level_field.shape[1], level_field.shape[2]) + downward(
            local_field
        )
    local_field = lax.dynamic_slice(
        local_field,
        (0, lax.axis_index("level") * coarse_y, lax.axis_index("cell") * coarse_x),
        (channels, coarse_y, coarse_x),
    )
    for k in range(HALO_LEVELS - 1, -1, -1):
        level_field = owned[k]
        local_field = grouped_far(
            framed_levels[k], 3, level_field.shape[1], level_field.shape[2]
        ) + downward(local_field)
    shifted = jnp.stack([framed[:, :, :, d : d + cells_x] for d in range(3)])
    return near_and_far(shifted, particles, local_field)


def solution(mesh):
    return jax.shard_map(
        local,
        mesh=mesh,
        in_specs=(
            P(None, "rep", "level", "cell"),
            P("rep", "level", "cell"),
            P(None, "rep", "level", "cell"),
            P("rep", "level", "cell"),
            P("rep", "level", "cell"),
            P("rep", "level", "cell"),
            P("rep", "level", "cell"),
        ),
        out_specs=P(None, "rep", "level", "cell"),
        check_vma=False,
    )
```

```python
import functools
import math

import jax
import jax.numpy as jnp
import numpy as np
from jax import lax
from jax.experimental import pallas as pl
from jax.experimental.pallas import tpu as pltpu
from jax.sharding import PartitionSpec as P

ORDER = 10
HALO_LEVELS = 4
CAP = 1024
BAND = 8
GROUP = 8
FRONT = 8


precise = lax.Precision.HIGHEST
blob_square = 0.09


def real_form(matrix):
    top_rows = np.concatenate([matrix.real, -matrix.imag], axis=1)
    low_rows = np.concatenate([matrix.imag, matrix.real], axis=1)
    return np.concatenate([top_rows, low_rows], axis=0)


def child_offset(parity_x, parity_y):
    return complex((parity_x - 0.5) / 2.0, (parity_y - 0.5) / 2.0)


def upward_table(parity_x, parity_y):
    offset = child_offset(parity_x, parity_y)
    matrix = np.zeros((ORDER, ORDER), complex)
    for k in range(ORDER):
        for m in range(k + 1):
            matrix[k, m] = math.comb(k, m) * 0.5**m * offset ** (k - m)
    return real_form(matrix)


def downward_table(parity_x, parity_y):
    offset = child_offset(parity_x, parity_y)
    matrix = np.zeros((ORDER, ORDER), complex)
    for m in range(ORDER):
        for l in range(m, ORDER):
            matrix[m, l] = 0.5 ** (m + 1) * math.comb(l, m) * offset ** (l - m)
    return real_form(matrix)


def far_table(step_x, step_y):
    distance = complex(step_x, step_y)
    matrix = np.zeros((ORDER, ORDER), complex)
    for l in range(ORDER):
        for k in range(ORDER):
            matrix[l, k] = (-1) ** (k + 1) * math.comb(k + l, l) * distance ** (-(k + l + 1))
    return real_form(matrix)


CHANNELS = 2 * ORDER
PITCH = 24
HIGH = dict(precision=lax.Precision.HIGHEST, preferred_element_type=jnp.float32)


def pack_starts(cells_y):
    starts = [0]
    for k in range(HALO_LEVELS):
        used = CHANNELS * (cells_y >> k)
        starts.append(starts[-1] + -(-used // 128) * 128)
    return starts


def upward_matrix():
    blocks = [upward_table(px, py) for px in (0, 1) for py in (0, 1)]
    matrix = np.zeros((PITCH, 4 * CHANNELS), np.float32)
    matrix[:CHANNELS] = np.concatenate(blocks, axis=1)
    return matrix


def level_matrix():
    matrix = np.zeros((4 * CHANNELS, 7 * 6 * CHANNELS + 2 * PITCH))
    for px in (0, 1):
        for py in (0, 1):
            rows = slice((2 * px + py) * CHANNELS, (2 * px + py + 1) * CHANNELS)
            for step_x in range(-2 - px, 4 - px):
                for step_y in range(-2 - py, 4 - py):
                    if max(abs(step_x), abs(step_y)) <= 1:
                        continue
                    first = ((step_x + 3) * 6 + step_y + py + 2) * CHANNELS
                    matrix[rows, first : first + CHANNELS] = far_table(step_x, step_y)
            first = 42 * CHANNELS + px * PITCH
            matrix[rows, first : first + CHANNELS] = downward_table(px, py)
    high = np.asarray(matrix, np.float32).astype(jnp.bfloat16)
    low = (matrix - high.astype(np.float64)).astype(np.float32).astype(jnp.bfloat16)
    return np.concatenate([high, low], axis=0)


def top_steps(cells):
    return [d for d in range(1 - cells, cells) if abs(d) >= 2]


def top_matrix(cells):
    steps = top_steps(cells)
    matrix = np.zeros((PITCH, PITCH * len(steps)), np.float32)
    for i, step in enumerate(steps):
        matrix[:CHANNELS, i * PITCH : i * PITCH + CHANNELS] = far_table(step, 0)
    return matrix


def lanes_of(shape):
    return lax.broadcasted_iota(jnp.int32, shape, len(shape) - 1)


def shifted_lanes(value, halo, distance):
    width = value.shape[-1]
    if distance == 0:
        return value
    lane = lanes_of(value.shape)
    if distance > 0:
        return pltpu.roll(jnp.where(lane < distance, halo, value), width - distance, value.ndim - 1)
    return pltpu.roll(jnp.where(lane >= width + distance, halo, value), -distance, value.ndim - 1)


def raise_level(matrix, level_value, cells_y, stride):
    wide = level_value.shape[-1]
    parts = []
    for row in range(cells_y // 2):
        here = level_value[2 * CHANNELS * row : 2 * CHANNELS * (row + 1)]
        parts.append(jnp.concatenate([here, pltpu.roll(here, wide - stride, 1)], axis=0))
    product = jnp.dot(matrix, jnp.concatenate(parts, axis=1), **HIGH)
    return [product[:CHANNELS, wide * row : wide * (row + 1)] for row in range(cells_y // 2)]


def upward_kernel(place_ref, own_ref, other_ref, up_ref, zero_ref, one_ref, two_ref, three_ref, four_ref, pack_ref):
    slots, cells_y, cells_x = own_ref.shape[1:]
    levels = [zero_ref, one_ref, two_ref, three_ref]
    for row in range(0, cells_y, BAND):
        here = pl.ds(row, BAND)

        def one_slot(s, sums):
            sums = list(sums)
            for parts_ref in (own_ref, other_ref):
                pos_x, pos_y = parts_ref[0, s, here, :], parts_ref[1, s, here, :]
                real, imag = parts_ref[2, s, here, :], jnp.zeros_like(pos_x)
                for k in range(ORDER):
                    sums[k] = sums[k] + real
                    sums[ORDER + k] = sums[ORDER + k] + imag
                    real, imag = real * pos_x - imag * pos_y, real * pos_y + imag * pos_x
            return tuple(sums)

        zero = jnp.zeros((BAND, cells_x), jnp.float32)
        sums = lax.fori_loop(0, slots, one_slot, (zero,) * CHANNELS)
        for c in range(CHANNELS):
            zero_ref[pl.ds(row * CHANNELS + c, BAND, stride=CHANNELS), :] = sums[c]
    up = up_ref[...]
    pack_ref[...] = jnp.zeros_like(pack_ref)
    starts = pack_starts(cells_y)
    for k in range(HALO_LEVELS):
        count = cells_y >> k
        value = levels[k][...]
        raised = raise_level(up, value, count, 1 << k)
        if k < HALO_LEVELS - 1:
            for row, piece in enumerate(raised):
                levels[k + 1][row * CHANNELS : (row + 1) * CHANNELS, :] = piece
        else:
            lane = lanes_of((cells_x, cells_x))
            source = lax.broadcasted_iota(jnp.int32, (cells_x, cells_x), 0)
            width = cells_x >> HALO_LEVELS
            wanted = (lane - place_ref[0] * width) * (1 << HALO_LEVELS)
            choose = ((source == wanted) & (wanted >= 0)).astype(jnp.float32)
            four = jnp.concatenate(raised, axis=0)
            four_ref[...] = jnp.dot(four, choose, **HIGH)
        which = lax.broadcasted_iota(jnp.int32, (8, cells_x), 0)
        pick = (lanes_of((8, cells_x)) == edge_lane(which, k, cells_x)).astype(jnp.float32)
        pack_ref[:, starts[k] : starts[k] + count * CHANNELS] = lax.dot_general(
            pick, value, (((1,), (1,)), ((), ())), **HIGH
        )


def edge_lane(which, k, cells_x):
    near = which * (1 << k)
    far = cells_x + (which - 4) * (1 << k)
    return jnp.where(which < 2, near, jnp.where(which < 4, far, -1))


def far_rows(matrix_ref, source_ref, halo_ref, count, stride, parent_ref, out_ref, stage_ref):
    wide = source_ref.shape[-1]
    rows = 6 * CHANNELS
    outer = count // 2
    chunk = min(outer, 4)

    def one_chunk(index, carry):
        for j in range(chunk):
            row = index * chunk + j
            begin = row * 2 * CHANNELS
            if not isinstance(begin, int):
                begin = pl.multiple_of(begin, 8)
            here = pl.ds(begin, rows)
            value = source_ref[here, :]
            halo = 0.0 if halo_ref is None else halo_ref[here, :]
            lanes = slice(j * wide, (j + 1) * wide)
            for step in range(-3, 4):
                first = (step + 3) * rows
                stage_ref[first : first + rows, lanes] = shifted_lanes(value, halo, step * stride)
            above = row * PITCH
            if not isinstance(above, int):
                above = pl.multiple_of(above, 8)
            parent = parent_ref[pl.ds(above, PITCH), :]
            stage_ref[7 * rows : 7 * rows + PITCH, lanes] = parent
            stage_ref[7 * rows + PITCH :, lanes] = pltpu.roll(parent, stride, 1)
        full = stage_ref[:, : chunk * wide]
        high = full.astype(jnp.bfloat16)
        low = (full - high.astype(jnp.float32)).astype(jnp.bfloat16)
        both = jnp.dot(matrix_ref[...], high, preferred_element_type=jnp.float32)
        rest = jnp.dot(matrix_ref[: 4 * CHANNELS, :], low, preferred_element_type=jnp.float32)
        total = both[: 4 * CHANNELS] + (both[4 * CHANNELS :] + rest)
        lane = lanes_of((2 * CHANNELS, wide))
        odd = lax.rem(lane // stride, 2) == 1
        for j in range(chunk):
            lanes = slice(j * wide, (j + 1) * wide)
            chosen = jnp.where(odd, total[2 * CHANNELS :, lanes], total[: 2 * CHANNELS, lanes])
            for py in (0, 1):
                begin = (2 * (index * chunk + j) + py) * PITCH
                if not isinstance(begin, int):
                    begin = pl.multiple_of(begin, 8)
                out_ref[pl.ds(begin, CHANNELS), :] = chosen[py * CHANNELS : (py + 1) * CHANNELS]
        return carry

    if outer == chunk:
        one_chunk(0, 0)
    else:
        lax.fori_loop(0, outer // chunk, one_chunk, 0)


def downward_kernel(
    place_ref, *refs, cells_y, cells_x, coarse_rows, coarse_cells
):
    owned = refs[:HALO_LEVELS]
    (before_ref, after_ref, packs_ref, coarse_ref, matrix_ref, up_ref, top_ref) = refs[4:11]
    near_ref, own_ref, out_ref = refs[11:14]
    scratch = list(refs[14:])
    padded, halos, fields = scratch[:4], scratch[4:8], scratch[8:12]
    stage_ref = scratch[12]
    coarse, coarse_fields = scratch[13:17], scratch[17:21]
    entry_ref = scratch[21]
    for ref in fields + coarse + coarse_fields + [entry_ref]:
        ref[...] = jnp.zeros_like(ref)
    edge = 2 * CHANNELS
    total = coarse_ref[0]
    for i in range(1, coarse_ref.shape[0]):
        total = total + coarse_ref[i]
    count = coarse_rows
    level = 0
    up = up_ref[...]
    value = total
    while True:
        coarse[level][edge : edge + count * CHANNELS, :] = value
        if count == 1:
            break
        value = jnp.concatenate(raise_level(up, value, count, 1 << level), axis=0)
        count //= 2
        level += 1
    stride = 1 << level
    steps = top_steps(coarse_cells >> level)
    if steps:
        base = coarse[level][edge : edge + PITCH, :]
        pieces = [shifted_lanes(base, 0.0, d * stride) for d in steps]
        coarse_fields[level][:PITCH, :] = jnp.dot(
            top_ref[...], jnp.concatenate(pieces, axis=0), **HIGH
        )
    while level > 0:
        level -= 1
        count *= 2
        far_rows(
            matrix_ref, coarse[level], None, count, 1 << level,
            coarse_fields[level + 1], coarse_fields[level], stage_ref,
        )
    rows_here = cells_y >> HALO_LEVELS
    width = cells_x >> HALO_LEVELS
    mine = coarse_fields[0][pl.ds(pl.multiple_of(place_ref[1] * rows_here * PITCH, 8), rows_here * PITCH), :]
    lane = lanes_of((cells_x, cells_x))
    source = lax.broadcasted_iota(jnp.int32, (cells_x, cells_x), 0)
    wanted = (source - place_ref[0] * width) * (1 << HALO_LEVELS)
    choose = ((lane == wanted) & (wanted >= 0)).astype(jnp.float32)
    entry_ref[...] = jnp.dot(mine, choose, **HIGH)
    starts = pack_starts(cells_y)
    across = []
    for i in range(3):
        across.append(packs_ref[i].T)
    for k in range(HALO_LEVELS - 1, -1, -1):
        count = cells_y >> k
        used = count * CHANNELS
        padded[k][:edge, :] = before_ref[k * edge : (k + 1) * edge, :]
        padded[k][edge : edge + used, :] = owned[k][...]
        padded[k][edge + used :, :] = after_ref[k * edge : (k + 1) * edge, :]
        which = lax.broadcasted_iota(jnp.int32, (8, cells_x), 0)
        spread = (lanes_of((8, cells_x)) == edge_lane(which, k, cells_x)).astype(jnp.float32)
        begin, end = starts[k], starts[k] + used
        halos[k][:edge, :] = jnp.dot(across[0][end - edge : end], spread, **HIGH)
        halos[k][edge : edge + used, :] = jnp.dot(across[1][begin:end], spread, **HIGH)
        halos[k][edge + used :, :] = jnp.dot(across[2][begin : begin + edge], spread, **HIGH)
        far_rows(
            matrix_ref, padded[k], halos[k], count, 1 << k,
            entry_ref if k == HALO_LEVELS - 1 else fields[k + 1], fields[k], stage_ref,
        )
    half_slots = own_ref.shape[1]
    scale = 1.0 / (2.0 * math.pi)
    for row in range(0, cells_y, BAND):
        here = pl.ds(row, BAND)

        def one_slot(t, carry):
            pos_x, pos_y = own_ref[0, t, here, :], own_ref[1, t, here, :]
            coefs = [
                fields[0][pl.ds(row * PITCH + c, BAND, stride=PITCH), :] for c in range(CHANNELS)
            ]
            real, imag = coefs[ORDER - 1], coefs[2 * ORDER - 1]
            for l in range(ORDER - 2, -1, -1):
                real, imag = (
                    real * pos_x - imag * pos_y + coefs[l],
                    real * pos_y + imag * pos_x + coefs[ORDER + l],
                )
            out_ref[0, t, here, :] = (imag + near_ref[1, t, here, :]) * scale
            out_ref[1, t, here, :] = (real + near_ref[0, t, here, :]) * scale
            return carry

        lax.fori_loop(0, half_slots, one_slot, 0)


VMEM = pl.BlockSpec(memory_space=pltpu.VMEM)
SMEM = pl.BlockSpec(memory_space=pltpu.SMEM)
PARAMS = pltpu.CompilerParams(vmem_limit_bytes=48 * 1024 * 1024)


def climb(place, own, other):
    cells_y, cells_x = own.shape[2:]
    shapes = [(CHANNELS * (cells_y >> k), cells_x) for k in range(HALO_LEVELS + 1)]
    shapes.append((8, pack_starts(cells_y)[-1]))
    return pl.pallas_call(
        upward_kernel,
        out_shape=[jax.ShapeDtypeStruct(s, jnp.float32) for s in shapes],
        in_specs=[SMEM, VMEM, VMEM, VMEM],
        out_specs=[VMEM] * len(shapes),
        compiler_params=PARAMS,
        name="climb",
    )(place, own, other, jnp.asarray(upward_matrix()))


def descend(place, owned, before, after, packs, coarse, near, own, coarse_cells):
    cells_y, cells_x = own.shape[2:]
    coarse_rows = coarse.shape[1] // CHANNELS
    levels = coarse_rows.bit_length()
    top = top_matrix(coarse_cells >> (levels - 1))
    matrix = level_matrix()
    edge = 2 * CHANNELS
    scratch = []
    for extra in range(2):
        for k in range(HALO_LEVELS):
            scratch.append((CHANNELS * (cells_y >> k) + 2 * edge, cells_x))
    for k in range(HALO_LEVELS):
        scratch.append((PITCH * (cells_y >> k), cells_x))
    scratch.append((matrix.shape[1], 4 * cells_x))
    for k in range(levels):
        scratch.append((CHANNELS * (coarse_rows >> k) + 2 * edge, cells_x))
    for k in range(levels):
        scratch.append((PITCH * max(coarse_rows >> k, 1), cells_x))
    scratch.append((PITCH * (cells_y >> HALO_LEVELS), cells_x))
    return pl.pallas_call(
        functools.partial(
            downward_kernel,
            cells_y=cells_y,
            cells_x=cells_x,
            coarse_rows=coarse_rows,
            coarse_cells=coarse_cells,
        ),
        out_shape=jax.ShapeDtypeStruct((2,) + own.shape[1:], jnp.float32),
        in_specs=[SMEM] + [VMEM] * 13,
        out_specs=VMEM,
        scratch_shapes=[pltpu.VMEM(s, jnp.float32) for s in scratch],
        compiler_params=PARAMS,
        name="descend",
    )(
        place, *owned, before, after, packs, coarse, jnp.asarray(matrix),
        jnp.asarray(upward_matrix()), jnp.asarray(top), near, own,
    )


MESH = pl.DeviceIdType.MESH


def greet(partners):
    barrier = pltpu.get_barrier_semaphore()
    count = jnp.int32(0)
    for present, device in partners:
        if present is None:
            pl.semaphore_signal(barrier, inc=1, device_id=device, device_id_type=MESH)
            count = count + 1
        else:

            @pl.when(present)
            def _():
                pl.semaphore_signal(barrier, inc=1, device_id=device, device_id_type=MESH)

            count = count + present.astype(jnp.int32)
    pl.semaphore_wait(barrier, count)


def position(offset, cells, levels, sign):
    c = lax.axis_index("cell") + sign * offset[0]
    l = lax.axis_index("level") + sign * offset[1]
    r = lax.axis_index("rep")
    r = 1 - r if offset[2] else r
    present = None
    if offset[0] or offset[1]:
        present = (c >= 0) & (c < cells) & (l >= 0) & (l < levels)
    return present, (c, l, r)


def guarded(present, action):
    if present is None:
        action()
    else:
        pl.when(present)(action)


def exchange_kernel(*refs, cells, levels, messages, inputs):
    sources, outs, (send_sem, recv_sem) = refs[:inputs], refs[inputs:-2], refs[-2:]
    offsets = sorted({offset for _, offset in messages})
    greet([position(offset, cells, levels, 1) for offset in offsets])

    def copy(i, device):
        return pltpu.make_async_remote_copy(
            src_ref=sources[messages[i][0]],
            dst_ref=outs[i],
            send_sem=send_sem.at[i],
            recv_sem=recv_sem.at[i],
            device_id=device,
            device_id_type=MESH,
        )

    for i, (_, offset) in enumerate(messages):
        present, device = position(offset, cells, levels, -1)
        guarded(present, lambda i=i, device=device: copy(i, device).start())
    for i, (_, offset) in enumerate(messages):
        present, device = position(offset, cells, levels, -1)
        guarded(present, lambda i=i, device=device: copy(i, device).wait_send())
        present, device = position(offset, cells, levels, 1)
        guarded(present, lambda i=i, device=device: copy(i, device).wait_recv())
        if present is not None:

            @pl.when(jnp.logical_not(present))
            def _(i=i):
                outs[i][...] = jnp.zeros_like(outs[i])


def exchange(arrays, messages, number, name):
    cells, levels = lax.axis_size("cell"), lax.axis_size("level")
    return pl.pallas_call(
        functools.partial(
            exchange_kernel, cells=cells, levels=levels, messages=messages, inputs=len(arrays)
        ),
        out_shape=[jax.ShapeDtypeStruct(arrays[i].shape, jnp.float32) for i, _ in messages],
        in_specs=[VMEM] * len(arrays),
        out_specs=[VMEM] * len(messages),
        scratch_shapes=[pltpu.SemaphoreType.DMA((len(messages),))] * 2,
        compiler_params=pltpu.CompilerParams(
            collective_id=number, has_side_effects=True, vmem_limit_bytes=48 * 1024 * 1024
        ),
        name=name,
    )(*arrays)


def spread_kernel(mine_ref, out_ref, send_sem, recv_sem, *, cells, levels, by_target):
    c, l, r = lax.axis_index("cell"), lax.axis_index("level"), lax.axis_index("rep")
    turns = [(i, j) for i in range(cells) for j in range(1 if by_target else levels) if i or j]

    def device(turn, sign):
        return (
            lax.rem(c + sign * turn[0] + cells, cells),
            lax.rem(l + sign * turn[1] + levels, levels),
            r,
        )

    def place(at):
        if by_target:
            return out_ref.at[at[0]]
        rows = mine_ref.shape[0]
        return out_ref.at[at[0], pl.ds(pl.multiple_of(at[1] * rows, 8), rows)]

    def copy(i, source, target):
        return pltpu.make_async_remote_copy(
            src_ref=mine_ref.at[target[0]] if by_target else mine_ref,
            dst_ref=place(source),
            send_sem=send_sem.at[i],
            recv_sem=recv_sem.at[i],
            device_id=target,
            device_id_type=MESH,
        )

    greet([(None, device(turn, 1)) for turn in turns])
    for i, turn in enumerate(turns):
        copy(i, (c, l, r), device(turn, 1)).start()
    if by_target:
        out_ref[c] = mine_ref[c]
    else:
        rows = mine_ref.shape[0]
        out_ref[c, pl.ds(pl.multiple_of(l * rows, 8), rows), :] = mine_ref[...]
    for i, turn in enumerate(turns):
        copy(i, (c, l, r), device(turn, 1)).wait_send()
        copy(i, device(turn, -1), (c, l, r)).wait_recv()


def spread(mine, number, by_target, name):
    cells, levels = lax.axis_size("cell"), lax.axis_size("level")
    shape = mine.shape if by_target else (cells, levels * mine.shape[0], mine.shape[1])
    count = cells * (1 if by_target else levels) - 1
    return pl.pallas_call(
        functools.partial(spread_kernel, cells=cells, levels=levels, by_target=by_target),
        out_shape=jax.ShapeDtypeStruct(shape, jnp.float32),
        in_specs=[VMEM],
        out_specs=VMEM,
        scratch_shapes=[pltpu.SemaphoreType.DMA((count,))] * 2,
        compiler_params=pltpu.CompilerParams(collective_id=number, has_side_effects=True),
        name=name,
    )(mine)


LANES = 128
PER_CHUNK = 8


def three_parts(value):
    high = value.astype(jnp.bfloat16).astype(jnp.float32)
    middle = (value - high).astype(jnp.bfloat16).astype(jnp.float32)
    return [high, middle, (value - high) - middle]


def one_hot_rows(index_row, rows):
    return lax.broadcasted_iota(jnp.int32, (rows, LANES), 0) == index_row


def stage_movers(a_ref, b_ref, j, row, lane, parts):
    lanes = slice(j * LANES, (j + 1) * LANES)
    a_ref[:, lanes] = jnp.where(one_hot_rows(row, a_ref.shape[0]), 1.0, 0.0).astype(jnp.bfloat16)
    at = one_hot_rows(lane, LANES)
    for p, part in enumerate(parts):
        b_ref[p * LANES : (p + 1) * LANES, lanes] = jnp.where(at, part, 0.0).astype(jnp.bfloat16)


def multiply_staged(a_ref, b_ref):
    return lax.dot_general(
        a_ref[...], b_ref[...], (((1,), (1,)), ((), ())), preferred_element_type=jnp.float32
    )


def pack_kernel(pos_ref, strength_ref, owner_ref, leaf_ref, slot_ref, out_ref, a_ref, b_ref, acc_ref, *, leaves):
    cells = out_ref.shape[0]
    owner = owner_ref[...]
    rows = owner.shape[0]
    first = lax.broadcasted_iota(jnp.int32, (LANES, LANES), 0)
    upto = jnp.where(first <= lanes_of((LANES, LANES)), 1.0, 0.0).astype(jnp.bfloat16)
    ones = jnp.ones((LANES, LANES), jnp.bfloat16)
    before = lax.broadcasted_iota(jnp.int32, (rows, rows), 0) > lanes_of((rows, rows))
    before = jnp.where(before, 1.0, 0.0).astype(jnp.bfloat16)
    dest = jnp.zeros(owner.shape, jnp.float32)
    for o in range(cells):
        mask = jnp.where(owner == o, 1.0, 0.0)
        narrow = mask.astype(jnp.bfloat16)
        inside = jnp.dot(narrow, upto, preferred_element_type=jnp.float32)
        above = jnp.dot(before, narrow, preferred_element_type=jnp.float32).astype(jnp.bfloat16)
        above = jnp.dot(above, ones, preferred_element_type=jnp.float32)
        dest = dest + mask * (inside + above + float(o * CAP - 1))
    dest = dest.astype(jnp.int32)
    address = slot_ref[...] * leaves + leaf_ref[...]
    parts = three_parts(pos_ref[0]) + three_parts(pos_ref[1]) + three_parts(strength_ref[...])
    parts.append(((address >> 8) + 1).astype(jnp.float32))
    parts.append((address & 255).astype(jnp.float32))
    to_row, to_lane = dest >> 7, dest & 127
    for chunk in range(rows // PER_CHUNK):
        for j in range(PER_CHUNK):
            row = slice(chunk * PER_CHUNK + j, chunk * PER_CHUNK + j + 1)
            stage_movers(a_ref, b_ref, j, to_row[row], to_lane[row], [p[row] for p in parts])
        product = multiply_staged(a_ref, b_ref)
        acc_ref[...] = product if chunk == 0 else acc_ref[...] + product
    for v in range(4):
        if v < 3:
            block = [acc_ref[:, (3 * v + p) * LANES : (3 * v + p + 1) * LANES] for p in range(3)]
            value = (block[0] + block[1]) + block[2]
        else:
            value = (acc_ref[:, 9 * LANES : 10 * LANES] - 1.0) * 256.0 + acc_ref[:, 10 * LANES :]
        for c in range(cells):
            out_ref[c, v * 8 : (v + 1) * 8, :] = value[c * 8 : (c + 1) * 8]


def pack_movers(pos, strength, owner, leaf, slot, leaves, cells):
    rows = strength.shape[0]
    return pl.pallas_call(
        functools.partial(pack_kernel, leaves=leaves),
        out_shape=jax.ShapeDtypeStruct((cells, 32, LANES), jnp.float32),
        in_specs=[VMEM] * 5,
        out_specs=VMEM,
        scratch_shapes=[
            pltpu.VMEM((cells * 8, PER_CHUNK * LANES), jnp.bfloat16),
            pltpu.VMEM((11 * LANES, PER_CHUNK * LANES), jnp.bfloat16),
            pltpu.VMEM((cells * 8, 11 * LANES), jnp.float32),
        ],
        compiler_params=PARAMS,
        name="pack_movers",
    )(pos, strength, owner, leaf, slot)


def settle_kernel(
    arrived_ref, pos_ref, strength_ref, out_ref, first_ref, last_ref, pack_ref, a_ref, b_ref, acc_ref
):
    half_slots, cells_y, cells_x = strength_ref.shape
    rows = half_slots * cells_y
    acc_ref[...] = jnp.zeros_like(acc_ref)

    def one_source(c, carry):
        place = arrived_ref[c, 24:32, :].astype(jnp.int32)
        to_row, to_lane = place >> 7, place & 127
        parts = []
        for v in range(3):
            parts += three_parts(arrived_ref[c, v * 8 : (v + 1) * 8, :])
        parts.append(jnp.ones_like(parts[0]))
        for j in range(PER_CHUNK):
            row = slice(j, j + 1)
            stage_movers(a_ref, b_ref, j, to_row[row], to_lane[row], [p[row] for p in parts])
        acc_ref[...] = acc_ref[...] + multiply_staged(a_ref, b_ref)
        return carry

    lax.fori_loop(0, arrived_ref.shape[0], one_source, 0)
    taken = acc_ref[:, 9 * LANES :] > 0.5
    packed = jnp.zeros(pack_ref.shape, jnp.float32)
    which = lax.broadcasted_iota(jnp.int32, (8, cells_x), 0)
    for v in range(3):
        block = [acc_ref[:, (3 * v + p) * LANES : (3 * v + p + 1) * LANES] for p in range(3)]
        old = (strength_ref[...] if v == 2 else pos_ref[v]).reshape(rows, cells_x)
        value = jnp.where(taken, (block[0] + block[1]) + block[2], old)
        out_ref[v] = value.reshape(half_slots, cells_y, cells_x)
        pick = (lanes_of((8, cells_x)) == side_lane(which, v, cells_x)).astype(jnp.float32)
        packed = packed + lax.dot_general(pick, value, (((1,), (1,)), ((), ())), **HIGH)
    pack_ref[...] = packed
    for v in range(3):
        for s in range(half_slots):
            row = v * half_slots + s
            first_ref[row : row + 1, :] = out_ref[v, s, 0:1, :]
            last_ref[row : row + 1, :] = out_ref[v, s, cells_y - 1 :, :]


def side_lane(which, v, cells_x):
    return jnp.where(which == v, 0, jnp.where(which == 4 + v, cells_x - 1, -1))


def settle(arrived, pos, strength):
    half_slots, cells_y, cells_x = strength.shape
    rows = half_slots * cells_y
    shapes = [(3,) + strength.shape, (3 * half_slots, cells_x), (3 * half_slots, cells_x), (8, rows)]
    return pl.pallas_call(
        settle_kernel,
        out_shape=[jax.ShapeDtypeStruct(s, jnp.float32) for s in shapes],
        in_specs=[VMEM] * 3,
        out_specs=[VMEM] * 4,
        scratch_shapes=[
            pltpu.VMEM((rows, PER_CHUNK * LANES), jnp.bfloat16),
            pltpu.VMEM((10 * LANES, PER_CHUNK * LANES), jnp.bfloat16),
            pltpu.VMEM((rows, 10 * LANES), jnp.float32),
        ],
        compiler_params=PARAMS,
        name="settle",
    )(arrived, pos, strength)


def near_kernel(own_ref, other_ref, before_ref, after_ref, packs_ref, out_ref, src_ref):
    half_slots, cells_y, cells_x = own_ref.shape[1:]
    slot_count = 2 * half_slots
    which = lax.broadcasted_iota(jnp.int32, (8, cells_x), 0)
    for half, ref in enumerate((own_ref, other_ref)):
        across = [packs_ref[half, i].T for i in range(3)]
        for v in range(3):
            pick = (lanes_of((8, cells_x)) == side_lane(which, v, cells_x)).astype(jnp.float32)
            halo = [jnp.dot(a, pick, **HIGH) for a in across]
            halo = [h.reshape(half_slots, cells_y, cells_x) for h in halo]
            rows = slice(v * half_slots, (v + 1) * half_slots)
            top, bottom = before_ref[half, rows, :], after_ref[half, rows, :]
            slots = slice(half * half_slots, (half + 1) * half_slots)
            for step in (-1, 0, 1):
                bias = float(step) if v == 0 else 0.0
                src_ref[step + 1, v, slots, FRONT : FRONT + cells_y, :] = (
                    shifted_lanes(ref[v], halo[1], step) + bias
                )
                up = shifted_lanes(top, halo[0][:, cells_y - 1, :], step) + bias
                down = shifted_lanes(bottom, halo[2][:, 0, :], step) + bias
                for s in range(half_slots):
                    slot = half * half_slots + s
                    src_ref[step + 1, v, slot, FRONT - 1 : FRONT, :] = up[s : s + 1]
                    src_ref[step + 1, v, slot, FRONT + cells_y : FRONT + cells_y + 1, :] = down[s : s + 1]

    def one_block(index, carry):
        row = pl.multiple_of((index // (half_slots // GROUP)) * BAND, BAND)
        slot = (index % (half_slots // GROUP)) * GROUP
        here = pl.ds(row, BAND)
        target_x = [own_ref[0, slot + t, here, :] for t in range(GROUP)]
        target_y = [own_ref[1, slot + t, here, :] for t in range(GROUP)]

        def one_source(s, sums):
            sums = list(sums)
            for step_y in (-1, 0, 1):
                there = pl.ds(row + FRONT + step_y, BAND)
                for step_x in (-1, 0, 1):
                    source_x = src_ref[step_x + 1, 0, s, there, :]
                    source_y = src_ref[step_x + 1, 1, s, there, :] + float(step_y)
                    strength = src_ref[step_x + 1, 2, s, there, :]
                    for t in range(GROUP):
                        gap_x = target_x[t] - source_x
                        gap_y = target_y[t] - source_y
                        square = gap_x * gap_x + (gap_y * gap_y + blob_square)
                        weight = strength * pl.reciprocal(square, approx=True)
                        sums[t] = sums[t] + weight * gap_x
                        sums[GROUP + t] = sums[GROUP + t] + weight * gap_y
            return tuple(sums)

        zero = jnp.zeros((BAND, cells_x), jnp.float32)
        sums = lax.fori_loop(0, slot_count, one_source, (zero,) * (2 * GROUP))
        for t in range(GROUP):
            out_ref[0, slot + t, here, :] = sums[t]
            out_ref[1, slot + t, here, :] = -sums[GROUP + t]
        return carry

    lax.fori_loop(0, (cells_y // BAND) * (half_slots // GROUP), one_block, 0)


def near_field(own, other, before, after, packs):
    half_slots, cells_y, cells_x = own.shape[1:]
    return pl.pallas_call(
        near_kernel,
        out_shape=jax.ShapeDtypeStruct((2,) + own.shape[1:], jnp.float32),
        in_specs=[VMEM] * 5,
        out_specs=VMEM,
        scratch_shapes=[
            pltpu.VMEM((3, 3, 2 * half_slots, cells_y + 2 * FRONT, cells_x), jnp.float32)
        ],
        compiler_params=PARAMS,
        name="near_field",
    )(own, other, before, after, packs)


def merged_sides(left, right):
    half = left.shape[-2] // 2
    return jnp.concatenate([right[..., :half, :], left[..., half:, :]], axis=-2)


def local(
    resident_pos, resident_strength, mover_pos, mover_strength, mover_owner, mover_leaf, mover_slot
):
    cells, levels = lax.axis_size("cell"), lax.axis_size("level")
    half_slots, cells_y, cells_x = resident_strength.shape
    place = jnp.stack([lax.axis_index("cell"), lax.axis_index("level")]).astype(jnp.int32)
    packed = pack_movers(
        mover_pos.reshape(2, -1, LANES),
        mover_strength.reshape(-1, LANES),
        mover_owner.reshape(-1, LANES),
        mover_leaf.reshape(-1, LANES),
        mover_slot.reshape(-1, LANES),
        cells_y * cells_x,
        cells,
    )
    arrived = spread(packed, 0, True, "send_movers")
    own, first, last, sides = settle(arrived, resident_pos, resident_strength)
    around = [(c, l) for l in (-1, 0, 1) for c in (-1, 1)]
    messages = [(0, (0, 0, 1))]
    for rep in (0, 1):
        messages += [(2, (0, -1, rep)), (1, (0, 1, rep))]
        messages += [(3, (c, l, rep)) for c, l in around]
    got = exchange([own, first, last, sides], messages, 1, "send_particles")
    other = got[0]
    by_rep = [got[1:9], got[9:17]]
    before = jnp.stack([g[0] for g in by_rep])
    after = jnp.stack([g[1] for g in by_rep])
    packs = jnp.stack(
        [
            jnp.stack([merged_sides(g[2 + 2 * i], g[3 + 2 * i]) for i in range(3)])
            for g in by_rep
        ]
    )
    climbed = climb(place, own, other)
    owned, mine, edges = climbed[:HALO_LEVELS], climbed[HALO_LEVELS], climbed[HALO_LEVELS + 1]
    edge = 2 * CHANNELS
    top_rows = jnp.concatenate([m[:edge] for m in owned])
    low_rows = jnp.concatenate([m[-edge:] for m in owned])
    messages = [(1, (0, -1, 0)), (0, (0, 1, 0))] + [(2, (c, l, 0)) for c, l in around]
    halo = exchange([top_rows, low_rows, edges], messages, 2, "send_multipoles")
    coarse = spread(mine, 3, False, "send_coarse")
    level_packs = jnp.stack([merged_edges(halo[2 + 2 * i], halo[3 + 2 * i]) for i in range(3)])
    near = near_field(own, other, before, after, packs)
    return descend(
        place, owned, halo[0], halo[1], level_packs, coarse, near, own,
        cells * (cells_x >> HALO_LEVELS),
    )


def merged_edges(left, right):
    return jnp.concatenate([right[:2], left[2:]], axis=0)


def solution(mesh):
    return jax.shard_map(
        local,
        mesh=mesh,
        in_specs=(
            P(None, "rep", "level", "cell"),
            P("rep", "level", "cell"),
            P(None, "rep", "level", "cell"),
            P("rep", "level", "cell"),
            P("rep", "level", "cell"),
            P("rep", "level", "cell"),
            P("rep", "level", "cell"),
        ),
        out_specs=P(None, "rep", "level", "cell"),
        check_vma=False,
    )
```

```python
import functools
import math

import jax
import jax.numpy as jnp
import numpy as np
from jax import lax
from jax.experimental import pallas as pl
from jax.experimental.pallas import tpu as pltpu
from jax.sharding import PartitionSpec as P

ORDER = 10
HALO_LEVELS = 4
CAP = 1024
BAND = 8
GROUP = 8
FRONT = 8


precise = lax.Precision.HIGHEST
blob_square = 0.09


def real_form(matrix):
    top_rows = np.concatenate([matrix.real, -matrix.imag], axis=1)
    low_rows = np.concatenate([matrix.imag, matrix.real], axis=1)
    return np.concatenate([top_rows, low_rows], axis=0)


def child_offset(parity_x, parity_y):
    return complex((parity_x - 0.5) / 2.0, (parity_y - 0.5) / 2.0)


def upward_table(parity_x, parity_y):
    offset = child_offset(parity_x, parity_y)
    matrix = np.zeros((ORDER, ORDER), complex)
    for k in range(ORDER):
        for m in range(k + 1):
            matrix[k, m] = math.comb(k, m) * 0.5**m * offset ** (k - m)
    return real_form(matrix)


def downward_table(parity_x, parity_y):
    offset = child_offset(parity_x, parity_y)
    matrix = np.zeros((ORDER, ORDER), complex)
    for m in range(ORDER):
        for l in range(m, ORDER):
            matrix[m, l] = 0.5 ** (m + 1) * math.comb(l, m) * offset ** (l - m)
    return real_form(matrix)


def far_table(step_x, step_y):
    distance = complex(step_x, step_y)
    matrix = np.zeros((ORDER, ORDER), complex)
    for l in range(ORDER):
        for k in range(ORDER):
            matrix[l, k] = (-1) ** (k + 1) * math.comb(k + l, l) * distance ** (-(k + l + 1))
    return real_form(matrix)


CHANNELS = 2 * ORDER
PITCH = 24
HIGH = dict(precision=lax.Precision.HIGHEST, preferred_element_type=jnp.float32)


def pack_starts(cells_y):
    starts = [0]
    for k in range(HALO_LEVELS):
        used = CHANNELS * (cells_y >> k)
        starts.append(starts[-1] + -(-used // 128) * 128)
    return starts


def upward_matrix():
    blocks = [upward_table(px, py) for px in (0, 1) for py in (0, 1)]
    matrix = np.zeros((PITCH, 4 * CHANNELS), np.float32)
    matrix[:CHANNELS] = np.concatenate(blocks, axis=1)
    return matrix


def level_matrix():
    matrix = np.zeros((4 * CHANNELS, 7 * 6 * CHANNELS + 2 * PITCH))
    for px in (0, 1):
        for py in (0, 1):
            rows = slice((2 * px + py) * CHANNELS, (2 * px + py + 1) * CHANNELS)
            for step_x in range(-2 - px, 4 - px):
                for step_y in range(-2 - py, 4 - py):
                    if max(abs(step_x), abs(step_y)) <= 1:
                        continue
                    first = ((step_x + 3) * 6 + step_y + py + 2) * CHANNELS
                    matrix[rows, first : first + CHANNELS] = far_table(step_x, step_y)
            first = 42 * CHANNELS + px * PITCH
            matrix[rows, first : first + CHANNELS] = downward_table(px, py)
    high = np.asarray(matrix, np.float32).astype(jnp.bfloat16)
    low = (matrix - high.astype(np.float64)).astype(np.float32).astype(jnp.bfloat16)
    return np.concatenate([high, low], axis=0)


def top_steps(cells):
    return [d for d in range(1 - cells, cells) if abs(d) >= 2]


def top_matrix(cells):
    steps = top_steps(cells)
    matrix = np.zeros((PITCH, PITCH * len(steps)), np.float32)
    for i, step in enumerate(steps):
        matrix[:CHANNELS, i * PITCH : i * PITCH + CHANNELS] = far_table(step, 0)
    return matrix


def lanes_of(shape):
    return lax.broadcasted_iota(jnp.int32, shape, len(shape) - 1)


def shifted_lanes(value, halo, distance):
    width = value.shape[-1]
    if distance == 0:
        return value
    lane = lanes_of(value.shape)
    if distance > 0:
        return pltpu.roll(jnp.where(lane < distance, halo, value), width - distance, value.ndim - 1)
    return pltpu.roll(jnp.where(lane >= width + distance, halo, value), -distance, value.ndim - 1)


def raise_level(matrix, level_value, cells_y, stride):
    wide = level_value.shape[-1]
    parts = []
    for row in range(cells_y // 2):
        here = level_value[2 * CHANNELS * row : 2 * CHANNELS * (row + 1)]
        parts.append(jnp.concatenate([here, pltpu.roll(here, wide - stride, 1)], axis=0))
    product = jnp.dot(matrix, jnp.concatenate(parts, axis=1), **HIGH)
    return [product[:CHANNELS, wide * row : wide * (row + 1)] for row in range(cells_y // 2)]


def climb_into(own_ref, other_ref, up_ref, zero_ref, one_ref, two_ref, three_ref, four_ref, pack_ref):
    slots, cells_y, cells_x = own_ref.shape[1:]
    levels = [zero_ref, one_ref, two_ref, three_ref]
    for row in range(0, cells_y, BAND):
        here = pl.ds(row, BAND)

        def one_slot(s, sums):
            sums = list(sums)
            for parts_ref in (own_ref, other_ref):
                pos_x, pos_y = parts_ref[0, s, here, :], parts_ref[1, s, here, :]
                real, imag = parts_ref[2, s, here, :], jnp.zeros_like(pos_x)
                for k in range(ORDER):
                    sums[k] = sums[k] + real
                    sums[ORDER + k] = sums[ORDER + k] + imag
                    real, imag = real * pos_x - imag * pos_y, real * pos_y + imag * pos_x
            return tuple(sums)

        zero = jnp.zeros((BAND, cells_x), jnp.float32)
        sums = lax.fori_loop(0, slots, one_slot, (zero,) * CHANNELS)
        for c in range(CHANNELS):
            zero_ref[pl.ds(row * CHANNELS + c, BAND, stride=CHANNELS), :] = sums[c]
    up = up_ref[...]
    pack_ref[...] = jnp.zeros_like(pack_ref)
    starts = pack_starts(cells_y)
    for k in range(HALO_LEVELS):
        count = cells_y >> k
        value = levels[k][...]
        raised = raise_level(up, value, count, 1 << k)
        if k < HALO_LEVELS - 1:
            for row, piece in enumerate(raised):
                levels[k + 1][row * CHANNELS : (row + 1) * CHANNELS, :] = piece
        else:
            lane = lanes_of((cells_x, cells_x))
            source = lax.broadcasted_iota(jnp.int32, (cells_x, cells_x), 0)
            width = cells_x >> HALO_LEVELS
            wanted = (lane - lax.axis_index("cell") * width) * (1 << HALO_LEVELS)
            choose = ((source == wanted) & (wanted >= 0)).astype(jnp.float32)
            four = jnp.concatenate(raised, axis=0)
            four_ref[...] = jnp.dot(four, choose, **HIGH)
        which = lax.broadcasted_iota(jnp.int32, (8, cells_x), 0)
        pick = (lanes_of((8, cells_x)) == edge_lane(which, k, cells_x)).astype(jnp.float32)
        pack_ref[:, starts[k] : starts[k] + count * CHANNELS] = lax.dot_general(
            pick, value, (((1,), (1,)), ((), ())), **HIGH
        )


def edge_lane(which, k, cells_x):
    near = which * (1 << k)
    far = cells_x + (which - 4) * (1 << k)
    return jnp.where(which < 2, near, jnp.where(which < 4, far, -1))


def far_rows(matrix_ref, source_ref, halo_ref, count, stride, parent_ref, out_ref, stage_ref):
    wide = source_ref.shape[-1]
    rows = 6 * CHANNELS
    outer = count // 2
    chunk = min(outer, 4)

    def one_chunk(index, carry):
        for j in range(chunk):
            row = index * chunk + j
            begin = row * 2 * CHANNELS
            if not isinstance(begin, int):
                begin = pl.multiple_of(begin, 8)
            here = pl.ds(begin, rows)
            value = source_ref[here, :]
            halo = 0.0 if halo_ref is None else halo_ref[here, :]
            lanes = slice(j * wide, (j + 1) * wide)
            for step in range(-3, 4):
                first = (step + 3) * rows
                stage_ref[first : first + rows, lanes] = shifted_lanes(value, halo, step * stride)
            above = row * PITCH
            if not isinstance(above, int):
                above = pl.multiple_of(above, 8)
            parent = parent_ref[pl.ds(above, PITCH), :]
            stage_ref[7 * rows : 7 * rows + PITCH, lanes] = parent
            stage_ref[7 * rows + PITCH :, lanes] = pltpu.roll(parent, stride, 1)
        full = stage_ref[:, : chunk * wide]
        high = full.astype(jnp.bfloat16)
        low = (full - high.astype(jnp.float32)).astype(jnp.bfloat16)
        both = jnp.dot(matrix_ref[...], high, preferred_element_type=jnp.float32)
        rest = jnp.dot(matrix_ref[: 4 * CHANNELS, :], low, preferred_element_type=jnp.float32)
        total = both[: 4 * CHANNELS] + (both[4 * CHANNELS :] + rest)
        lane = lanes_of((2 * CHANNELS, wide))
        odd = lax.rem(lane // stride, 2) == 1
        for j in range(chunk):
            lanes = slice(j * wide, (j + 1) * wide)
            chosen = jnp.where(odd, total[2 * CHANNELS :, lanes], total[: 2 * CHANNELS, lanes])
            for py in (0, 1):
                begin = (2 * (index * chunk + j) + py) * PITCH
                if not isinstance(begin, int):
                    begin = pl.multiple_of(begin, 8)
                out_ref[pl.ds(begin, CHANNELS), :] = chosen[py * CHANNELS : (py + 1) * CHANNELS]
        return carry

    if outer == chunk:
        one_chunk(0, 0)
    else:
        lax.fori_loop(0, outer // chunk, one_chunk, 0)


def downward_kernel(
    place_ref, *refs, cells_y, cells_x, coarse_rows, coarse_cells
):
    owned = refs[:HALO_LEVELS]
    before_ref, after_ref, sides = refs[4], refs[5], refs[6:12]
    coarse_ref, matrix_ref, up_ref, top_ref, near_ref, own_ref, out_ref = refs[12:19]
    scratch = list(refs[19:])
    padded, halos, fields = scratch[:4], scratch[4:8], scratch[8:12]
    stage_ref = scratch[12]
    coarse, coarse_fields = scratch[13:17], scratch[17:21]
    entry_ref = scratch[21]
    for ref in fields + coarse + coarse_fields + [entry_ref]:
        ref[...] = jnp.zeros_like(ref)
    edge = 2 * CHANNELS
    total = coarse_ref[0]
    for i in range(1, coarse_ref.shape[0]):
        total = total + coarse_ref[i]
    count = coarse_rows
    level = 0
    up = up_ref[...]
    value = total
    while True:
        coarse[level][edge : edge + count * CHANNELS, :] = value
        if count == 1:
            break
        value = jnp.concatenate(raise_level(up, value, count, 1 << level), axis=0)
        count //= 2
        level += 1
    stride = 1 << level
    steps = top_steps(coarse_cells >> level)
    if steps:
        base = coarse[level][edge : edge + PITCH, :]
        pieces = [shifted_lanes(base, 0.0, d * stride) for d in steps]
        coarse_fields[level][:PITCH, :] = jnp.dot(
            top_ref[...], jnp.concatenate(pieces, axis=0), **HIGH
        )
    while level > 0:
        level -= 1
        count *= 2
        far_rows(
            matrix_ref, coarse[level], None, count, 1 << level,
            coarse_fields[level + 1], coarse_fields[level], stage_ref,
        )
    rows_here = cells_y >> HALO_LEVELS
    width = cells_x >> HALO_LEVELS
    mine = coarse_fields[0][pl.ds(pl.multiple_of(place_ref[1] * rows_here * PITCH, 8), rows_here * PITCH), :]
    lane = lanes_of((cells_x, cells_x))
    source = lax.broadcasted_iota(jnp.int32, (cells_x, cells_x), 0)
    wanted = (source - place_ref[0] * width) * (1 << HALO_LEVELS)
    choose = ((lane == wanted) & (wanted >= 0)).astype(jnp.float32)
    entry_ref[...] = jnp.dot(mine, choose, **HIGH)
    starts = pack_starts(cells_y)
    across = []
    for i in range(3):
        across.append(merged_sides(sides[2 * i], sides[2 * i + 1], 2))
    for k in range(HALO_LEVELS - 1, -1, -1):
        count = cells_y >> k
        used = count * CHANNELS
        padded[k][:edge, :] = before_ref[k * edge : (k + 1) * edge, :]
        padded[k][edge : edge + used, :] = owned[k][...]
        padded[k][edge + used :, :] = after_ref[k * edge : (k + 1) * edge, :]
        which = lax.broadcasted_iota(jnp.int32, (8, cells_x), 0)
        spread = (lanes_of((8, cells_x)) == edge_lane(which, k, cells_x)).astype(jnp.float32)
        begin, end = starts[k], starts[k] + used
        halos[k][:edge, :] = jnp.dot(across[0][end - edge : end], spread, **HIGH)
        halos[k][edge : edge + used, :] = jnp.dot(across[1][begin:end], spread, **HIGH)
        halos[k][edge + used :, :] = jnp.dot(across[2][begin : begin + edge], spread, **HIGH)
        far_rows(
            matrix_ref, padded[k], halos[k], count, 1 << k,
            entry_ref if k == HALO_LEVELS - 1 else fields[k + 1], fields[k], stage_ref,
        )
    half_slots = own_ref.shape[1]
    scale = 1.0 / (2.0 * math.pi)
    for row in range(0, cells_y, BAND):
        here = pl.ds(row, BAND)

        def one_slot(t, carry):
            pos_x, pos_y = own_ref[0, t, here, :], own_ref[1, t, here, :]
            coefs = [
                fields[0][pl.ds(row * PITCH + c, BAND, stride=PITCH), :] for c in range(CHANNELS)
            ]
            real, imag = coefs[ORDER - 1], coefs[2 * ORDER - 1]
            for l in range(ORDER - 2, -1, -1):
                real, imag = (
                    real * pos_x - imag * pos_y + coefs[l],
                    real * pos_y + imag * pos_x + coefs[ORDER + l],
                )
            out_ref[0, t, here, :] = (imag + near_ref[1, t, here, :]) * scale
            out_ref[1, t, here, :] = (real + near_ref[0, t, here, :]) * scale
            return carry

        lax.fori_loop(0, half_slots, one_slot, 0)


VMEM = pl.BlockSpec(memory_space=pltpu.VMEM)
SMEM = pl.BlockSpec(memory_space=pltpu.SMEM)
PARAMS = pltpu.CompilerParams(vmem_limit_bytes=48 * 1024 * 1024)


def descend(place, owned, halo, coarse, near, own, coarse_cells):
    cells_y, cells_x = own.shape[2:]
    coarse_rows = coarse.shape[1] // CHANNELS
    levels = coarse_rows.bit_length()
    top = top_matrix(coarse_cells >> (levels - 1))
    matrix = level_matrix()
    edge = 2 * CHANNELS
    scratch = []
    for extra in range(2):
        for k in range(HALO_LEVELS):
            scratch.append((CHANNELS * (cells_y >> k) + 2 * edge, cells_x))
    for k in range(HALO_LEVELS):
        scratch.append((PITCH * (cells_y >> k), cells_x))
    scratch.append((matrix.shape[1], 4 * cells_x))
    for k in range(levels):
        scratch.append((CHANNELS * (coarse_rows >> k) + 2 * edge, cells_x))
    for k in range(levels):
        scratch.append((PITCH * max(coarse_rows >> k, 1), cells_x))
    scratch.append((PITCH * (cells_y >> HALO_LEVELS), cells_x))
    return pl.pallas_call(
        functools.partial(
            downward_kernel,
            cells_y=cells_y,
            cells_x=cells_x,
            coarse_rows=coarse_rows,
            coarse_cells=coarse_cells,
        ),
        out_shape=jax.ShapeDtypeStruct((2,) + own.shape[1:], jnp.float32),
        in_specs=[SMEM] + [VMEM] * 18,
        out_specs=VMEM,
        scratch_shapes=[pltpu.VMEM(s, jnp.float32) for s in scratch],
        compiler_params=PARAMS,
        name="descend",
    )(
        place, *owned, *halo, coarse, jnp.asarray(matrix),
        jnp.asarray(upward_matrix()), jnp.asarray(top), near, own,
    )


MESH = pl.DeviceIdType.MESH


def position(offset, cells, levels, sign):
    c = lax.axis_index("cell") + sign * offset[0]
    l = lax.axis_index("level") + sign * offset[1]
    r = lax.axis_index("rep")
    r = 1 - r if offset[2] else r
    present = None
    if offset[0] or offset[1]:
        present = (c >= 0) & (c < cells) & (l >= 0) & (l < levels)
    return present, (c, l, r)


def turned(turn, cells, levels, sign):
    return (
        lax.rem(lax.axis_index("cell") + sign * turn[0] + cells, cells),
        lax.rem(lax.axis_index("level") + sign * turn[1] + levels, levels),
        lax.axis_index("rep"),
    )


def guarded(present, action):
    if present is None:
        action()
    else:
        pl.when(present)(action)


def greet(partners):
    barrier = pltpu.get_barrier_semaphore()
    count = jnp.int32(0)
    for present, device in partners:

        def signal(device=device):
            pl.semaphore_signal(barrier, inc=1, device_id=device, device_id_type=MESH)

        guarded(present, signal)
        count = count + (1 if present is None else present.astype(jnp.int32))
    return lambda: pl.semaphore_wait(barrier, count)


class Exchange:
    def __init__(self, sources, outs, offsets, send_sem, recv_sem, cells, levels):
        self.sources, self.outs, self.offsets = sources, outs, offsets
        self.send_sem, self.recv_sem = send_sem, recv_sem
        self.grid = (cells, levels)

    def copy(self, i, device):
        return pltpu.make_async_remote_copy(
            src_ref=self.sources[i],
            dst_ref=self.outs[i],
            send_sem=self.send_sem.at[i],
            recv_sem=self.recv_sem.at[i],
            device_id=device,
            device_id_type=MESH,
        )

    def start(self):
        for i, offset in enumerate(self.offsets):
            present, device = position(offset, *self.grid, -1)
            guarded(present, lambda i=i, device=device: self.copy(i, device).start())

    def wait(self):
        for i, offset in enumerate(self.offsets):
            present, device = position(offset, *self.grid, -1)
            guarded(present, lambda i=i, device=device: self.copy(i, device).wait_send())
            present, device = position(offset, *self.grid, 1)
            guarded(present, lambda i=i, device=device: self.copy(i, device).wait_recv())
            if present is not None:

                @pl.when(jnp.logical_not(present))
                def _(i=i):
                    self.outs[i][...] = jnp.zeros_like(self.outs[i])


AROUND = [(c, l) for l in (-1, 0, 1) for c in (-1, 1)]


LANES = 128
PER_CHUNK = 8


def three_parts(value):
    high = value.astype(jnp.bfloat16).astype(jnp.float32)
    middle = (value - high).astype(jnp.bfloat16).astype(jnp.float32)
    return [high, middle, (value - high) - middle]


def one_hot_rows(index_row, rows):
    return lax.broadcasted_iota(jnp.int32, (rows, LANES), 0) == index_row


def stage_movers(a_ref, b_ref, j, row, lane, parts):
    lanes = slice(j * LANES, (j + 1) * LANES)
    a_ref[:, lanes] = jnp.where(one_hot_rows(row, a_ref.shape[0]), 1.0, 0.0).astype(jnp.bfloat16)
    at = one_hot_rows(lane, LANES)
    for p, part in enumerate(parts):
        b_ref[p * LANES : (p + 1) * LANES, lanes] = jnp.where(at, part, 0.0).astype(jnp.bfloat16)


def multiply_staged(a_ref, b_ref):
    return lax.dot_general(
        a_ref[...], b_ref[...], (((1,), (1,)), ((), ())), preferred_element_type=jnp.float32
    )


def pack_into(packed_ref, pos_ref, strength_ref, owner_ref, leaf_ref, slot_ref, a_ref, b_ref, acc_ref, leaves):
    cells = packed_ref.shape[0]
    owner = owner_ref[...]
    rows = owner.shape[0]
    first = lax.broadcasted_iota(jnp.int32, (LANES, LANES), 0)
    upto = jnp.where(first <= lanes_of((LANES, LANES)), 1.0, 0.0).astype(jnp.bfloat16)
    ones = jnp.ones((LANES, LANES), jnp.bfloat16)
    before = lax.broadcasted_iota(jnp.int32, (rows, rows), 0) > lanes_of((rows, rows))
    before = jnp.where(before, 1.0, 0.0).astype(jnp.bfloat16)
    dest = jnp.zeros(owner.shape, jnp.float32)
    for o in range(cells):
        mask = jnp.where(owner == o, 1.0, 0.0)
        narrow = mask.astype(jnp.bfloat16)
        inside = jnp.dot(narrow, upto, preferred_element_type=jnp.float32)
        above = jnp.dot(before, narrow, preferred_element_type=jnp.float32).astype(jnp.bfloat16)
        above = jnp.dot(above, ones, preferred_element_type=jnp.float32)
        dest = dest + mask * (inside + above + float(o * CAP - 1))
    dest = dest.astype(jnp.int32)
    address = slot_ref[...] * leaves + leaf_ref[...]
    parts = three_parts(pos_ref[0]) + three_parts(pos_ref[1]) + three_parts(strength_ref[...])
    parts.append(((address >> 8) + 1).astype(jnp.float32))
    parts.append((address & 255).astype(jnp.float32))
    to_row, to_lane = dest >> 7, dest & 127
    for chunk in range(rows // PER_CHUNK):
        for j in range(PER_CHUNK):
            row = slice(chunk * PER_CHUNK + j, chunk * PER_CHUNK + j + 1)
            stage_movers(a_ref, b_ref, j, to_row[row], to_lane[row], [p[row] for p in parts])
        product = multiply_staged(a_ref, b_ref)
        acc_ref[...] = product if chunk == 0 else acc_ref[...] + product
    for v in range(4):
        if v < 3:
            block = [acc_ref[:, (3 * v + p) * LANES : (3 * v + p + 1) * LANES] for p in range(3)]
            value = (block[0] + block[1]) + block[2]
        else:
            value = (acc_ref[:, 9 * LANES : 10 * LANES] - 1.0) * 256.0 + acc_ref[:, 10 * LANES :]
        for c in range(cells):
            packed_ref[c, v * 8 : (v + 1) * 8, :] = value[c * 8 : (c + 1) * 8]


def settle_chunk(arrived, a_ref, b_ref, acc_ref):
    place = arrived[24:32, :].astype(jnp.int32)
    to_row, to_lane = place >> 7, place & 127
    parts = []
    for v in range(3):
        parts += three_parts(arrived[v * 8 : (v + 1) * 8, :])
    parts.append(jnp.ones_like(parts[0]))
    for j in range(PER_CHUNK):
        row = slice(j, j + 1)
        stage_movers(a_ref, b_ref, j, to_row[row], to_lane[row], [p[row] for p in parts])
    acc_ref[...] = acc_ref[...] + multiply_staged(a_ref, b_ref)


def finish_settle(pos_ref, strength_ref, out_ref, first_ref, last_ref, pack_ref, acc_ref):
    half_slots, cells_y, cells_x = strength_ref.shape
    rows = half_slots * cells_y
    taken = acc_ref[:, 9 * LANES :] > 0.5
    packed = jnp.zeros(pack_ref.shape, jnp.float32)
    which = lax.broadcasted_iota(jnp.int32, (8, cells_x), 0)
    for v in range(3):
        block = [acc_ref[:, (3 * v + p) * LANES : (3 * v + p + 1) * LANES] for p in range(3)]
        old = (strength_ref[...] if v == 2 else pos_ref[v]).reshape(rows, cells_x)
        value = jnp.where(taken, (block[0] + block[1]) + block[2], old)
        out_ref[v] = value.reshape(half_slots, cells_y, cells_x)
        pick = (lanes_of((8, cells_x)) == side_lane(which, v, cells_x)).astype(jnp.float32)
        packed = packed + lax.dot_general(pick, value, (((1,), (1,)), ((), ())), **HIGH)
    pack_ref[...] = packed
    for v in range(3):
        for s in range(half_slots):
            row = v * half_slots + s
            first_ref[row : row + 1, :] = out_ref[v, s, 0:1, :]
            last_ref[row : row + 1, :] = out_ref[v, s, cells_y - 1 :, :]


def particle_offsets():
    offsets = [(0, 0, 1)]
    for rep in (0, 1):
        offsets += [(0, -1, rep), (0, 1, rep)] + [(c, l, rep) for c, l in AROUND]
    return offsets


def route_kernel(*refs, leaves, cells, levels):
    inputs, refs = refs[:7], refs[7:]
    own_ref, received, refs = refs[0], refs[1:18], refs[18:]
    held, refs = refs[:7], refs[7:]
    (
        packed_ref, arrived_ref, a_pack, b_pack, acc_pack, a_ref, b_ref, acc_ref,
        first_ref, last_ref, side_ref, load_sem, move_send, move_recv, send_sem, recv_sem,
    ) = refs
    offsets = particle_offsets()
    partners = [(None, turned((i, 0), cells, levels, 1)) for i in range(1, cells)]
    partners += [position(o, cells, levels, 1) for o in offsets if o[1] or o[2]]
    all_in = greet(partners)
    loads = [
        pltpu.make_async_copy(source, target, load_sem.at[i])
        for i, (source, target) in enumerate(zip(inputs, held))
    ]
    for load in loads:
        load.start()
    for load in loads[:5]:
        load.wait()
    pos_ref, strength_ref = held[5:]
    pack_into(packed_ref, *held[:5], a_pack, b_pack, acc_pack, leaves)
    acc_ref[...] = jnp.zeros_like(acc_ref)
    me = lax.axis_index("cell")
    all_in()

    def move(i):
        target = turned((i, 0), cells, levels, 1)
        return pltpu.make_async_remote_copy(
            src_ref=packed_ref.at[target[0]],
            dst_ref=arrived_ref.at[i],
            send_sem=move_send.at[i],
            recv_sem=move_recv.at[i],
            device_id=target,
            device_id_type=MESH,
        )

    for i in range(1, cells):
        move(i).start()
    arrived_ref[0] = packed_ref[me]
    settle_chunk(arrived_ref[0], a_ref, b_ref, acc_ref)

    def one_source(i, carry):
        move(i).wait_recv()
        settle_chunk(arrived_ref[i], a_ref, b_ref, acc_ref)
        return carry

    lax.fori_loop(1, cells, one_source, 0)
    for load in loads[5:]:
        load.wait()
    finish_settle(pos_ref, strength_ref, own_ref, first_ref, last_ref, side_ref, acc_ref)
    sources = [own_ref] + [last_ref, first_ref] + [side_ref] * 6 + [last_ref, first_ref] + [side_ref] * 6
    swap = Exchange(sources, received, offsets, send_sem, recv_sem, cells, levels)
    swap.start()
    for i in range(1, cells):
        move(i).wait_send()
    swap.wait()


def route(movers, pos, strength):
    cells, levels = lax.axis_size("cell"), lax.axis_size("level")
    half_slots, cells_y, cells_x = strength.shape
    rows = half_slots * cells_y
    own = (3,) + strength.shape
    edge, side = (3 * half_slots, cells_x), (8, rows)
    shapes = [own, own] + ([edge] * 2 + [side] * 6) * 2
    inputs = list(movers) + [pos, strength]
    wide = PER_CHUNK * LANES
    return pl.pallas_call(
        functools.partial(route_kernel, leaves=cells_y * cells_x, cells=cells, levels=levels),
        out_shape=[jax.ShapeDtypeStruct(s, jnp.float32) for s in shapes],
        in_specs=[pl.BlockSpec(memory_space=pl.ANY)] * len(inputs),
        out_specs=[VMEM] * len(shapes),
        scratch_shapes=[pltpu.VMEM(x.shape, x.dtype) for x in inputs]
        + [
            pltpu.VMEM((cells, 32, LANES), jnp.float32),
            pltpu.VMEM((cells, 32, LANES), jnp.float32),
            pltpu.VMEM((cells * 8, wide), jnp.bfloat16),
            pltpu.VMEM((11 * LANES, wide), jnp.bfloat16),
            pltpu.VMEM((cells * 8, 11 * LANES), jnp.float32),
            pltpu.VMEM((rows, wide), jnp.bfloat16),
            pltpu.VMEM((10 * LANES, wide), jnp.bfloat16),
            pltpu.VMEM((rows, 10 * LANES), jnp.float32),
            pltpu.VMEM(edge, jnp.float32),
            pltpu.VMEM(edge, jnp.float32),
            pltpu.VMEM(side, jnp.float32),
            pltpu.SemaphoreType.DMA((7,)),
            pltpu.SemaphoreType.DMA((cells,)),
            pltpu.SemaphoreType.DMA((cells,)),
            pltpu.SemaphoreType.DMA((17,)),
            pltpu.SemaphoreType.DMA((17,)),
        ],
        compiler_params=pltpu.CompilerParams(
            collective_id=0, has_side_effects=True, vmem_limit_bytes=56 * 1024 * 1024
        ),
        name="route",
    )(*inputs)


def side_lane(which, v, cells_x):
    return jnp.where(which == v, 0, jnp.where(which == 4 + v, cells_x - 1, -1))


def merged_sides(left_ref, right_ref, split):
    row = lax.broadcasted_iota(jnp.int32, left_ref.shape, 0)
    return jnp.where(row < split, right_ref[...], left_ref[...]).T


def near_into(out_ref, own_ref, other_ref, frames, src_ref):
    half_slots, cells_y, cells_x = own_ref.shape[1:]
    slot_count = 2 * half_slots
    which = lax.broadcasted_iota(jnp.int32, (8, cells_x), 0)
    for half, ref in enumerate((own_ref, other_ref)):
        before_ref, after_ref, sides = frames[half][0], frames[half][1], frames[half][2:]
        across = [merged_sides(sides[2 * i], sides[2 * i + 1], 4) for i in range(3)]
        for v in range(3):
            pick = (lanes_of((8, cells_x)) == side_lane(which, v, cells_x)).astype(jnp.float32)
            halo = [jnp.dot(a, pick, **HIGH) for a in across]
            halo = [h.reshape(half_slots, cells_y, cells_x) for h in halo]
            rows = slice(v * half_slots, (v + 1) * half_slots)
            top, bottom = before_ref[rows, :], after_ref[rows, :]
            slots = slice(half * half_slots, (half + 1) * half_slots)
            for step in (-1, 0, 1):
                bias = float(step) if v == 0 else 0.0
                src_ref[step + 1, v, slots, FRONT : FRONT + cells_y, :] = (
                    shifted_lanes(ref[v], halo[1], step) + bias
                )
                up = shifted_lanes(top, halo[0][:, cells_y - 1, :], step) + bias
                down = shifted_lanes(bottom, halo[2][:, 0, :], step) + bias
                for s in range(half_slots):
                    slot = half * half_slots + s
                    src_ref[step + 1, v, slot, FRONT - 1 : FRONT, :] = up[s : s + 1]
                    src_ref[step + 1, v, slot, FRONT + cells_y : FRONT + cells_y + 1, :] = down[s : s + 1]

    def one_block(index, carry):
        row = pl.multiple_of((index // (half_slots // GROUP)) * BAND, BAND)
        slot = (index % (half_slots // GROUP)) * GROUP
        here = pl.ds(row, BAND)
        target_x = [own_ref[0, slot + t, here, :] for t in range(GROUP)]
        target_y = [own_ref[1, slot + t, here, :] for t in range(GROUP)]

        def one_source(s, sums):
            sums = list(sums)
            for step_y in (-1, 0, 1):
                there = pl.ds(row + FRONT + step_y, BAND)
                for step_x in (-1, 0, 1):
                    source_x = src_ref[step_x + 1, 0, s, there, :]
                    source_y = src_ref[step_x + 1, 1, s, there, :] + float(step_y)
                    strength = src_ref[step_x + 1, 2, s, there, :]
                    for t in range(GROUP):
                        gap_x = target_x[t] - source_x
                        gap_y = target_y[t] - source_y
                        square = gap_x * gap_x + (gap_y * gap_y + blob_square)
                        weight = strength * pl.reciprocal(square, approx=True)
                        sums[t] = sums[t] + weight * gap_x
                        sums[GROUP + t] = sums[GROUP + t] + weight * gap_y
            return tuple(sums)

        zero = jnp.zeros((BAND, cells_x), jnp.float32)
        sums = lax.fori_loop(0, slot_count, one_source, (zero,) * (2 * GROUP))
        for t in range(GROUP):
            out_ref[0, slot + t, here, :] = sums[t]
            out_ref[1, slot + t, here, :] = -sums[GROUP + t]
        return carry

    lax.fori_loop(0, (cells_y // BAND) * (half_slots // GROUP), one_block, 0)


def climb_kernel(*refs, cells, levels):
    own_ref, other_ref, refs = refs[0], refs[1], refs[2:]
    frames, refs = [refs[:8], refs[8:16]], refs[16:]
    up_ref, refs = refs[0], refs[1:]
    owned, refs = refs[:HALO_LEVELS], refs[HALO_LEVELS:]
    received, coarse_ref, near_ref, refs = refs[:8], refs[8], refs[9], refs[10:]
    mine_ref, edges_ref, top_ref, low_ref, src_ref = refs[:5]
    send_sem, recv_sem, coarse_send, coarse_recv = refs[5:]
    turns = [(i, j) for i in range(cells) for j in range(levels) if i or j]
    all_in = greet([(None, turned(turn, cells, levels, 1)) for turn in turns])
    climb_into(own_ref, other_ref, up_ref, *owned, mine_ref, edges_ref)
    edge = 2 * CHANNELS
    for k in range(HALO_LEVELS):
        here = slice(k * edge, (k + 1) * edge)
        top_ref[here, :] = owned[k][:edge, :]
        low_ref[here, :] = owned[k][owned[k].shape[0] - edge :, :]
    offsets = [(0, -1, 0), (0, 1, 0)] + [(c, l, 0) for c, l in AROUND]
    sources = [low_ref, top_ref] + [edges_ref] * 6
    swap = Exchange(sources, received, offsets, send_sem, recv_sem, cells, levels)
    rows = mine_ref.shape[0]

    def copy(i, source, target):
        return pltpu.make_async_remote_copy(
            src_ref=mine_ref,
            dst_ref=coarse_ref.at[source[0], pl.ds(pl.multiple_of(source[1] * rows, 8), rows)],
            send_sem=coarse_send.at[i],
            recv_sem=coarse_recv.at[i],
            device_id=target,
            device_id_type=MESH,
        )

    me = turned((0, 0), cells, levels, 1)
    all_in()
    swap.start()
    for i, turn in enumerate(turns):
        copy(i, me, turned(turn, cells, levels, 1)).start()
    coarse_ref[me[0], pl.ds(pl.multiple_of(me[1] * rows, 8), rows), :] = mine_ref[...]
    near_into(near_ref, own_ref, other_ref, frames, src_ref)
    swap.wait()
    for i, turn in enumerate(turns):
        copy(i, me, turned(turn, cells, levels, 1)).wait_send()
        copy(i, turned(turn, cells, levels, -1), me).wait_recv()


def climb_and_near(own, other, frames):
    cells, levels = lax.axis_size("cell"), lax.axis_size("level")
    half_slots, cells_y, cells_x = own.shape[1:]
    owned = [(CHANNELS * (cells_y >> k), cells_x) for k in range(HALO_LEVELS)]
    mine = (CHANNELS * (cells_y >> HALO_LEVELS), cells_x)
    edges = (8, pack_starts(cells_y)[-1])
    rows = (2 * CHANNELS * HALO_LEVELS, cells_x)
    shapes = owned + [rows] * 2 + [edges] * 6
    shapes += [(cells, levels * mine[0], cells_x), (2,) + own.shape[1:]]
    inputs = [own, other, *frames, jnp.asarray(upward_matrix())]
    return pl.pallas_call(
        functools.partial(climb_kernel, cells=cells, levels=levels),
        out_shape=[jax.ShapeDtypeStruct(s, jnp.float32) for s in shapes],
        in_specs=[VMEM] * len(inputs),
        out_specs=[VMEM] * len(shapes),
        scratch_shapes=[
            pltpu.VMEM(mine, jnp.float32),
            pltpu.VMEM(edges, jnp.float32),
            pltpu.VMEM(rows, jnp.float32),
            pltpu.VMEM(rows, jnp.float32),
            pltpu.VMEM((3, 3, 2 * half_slots, cells_y + 2 * FRONT, cells_x), jnp.float32),
            pltpu.SemaphoreType.DMA((8,)),
            pltpu.SemaphoreType.DMA((8,)),
            pltpu.SemaphoreType.DMA((cells * levels - 1,)),
            pltpu.SemaphoreType.DMA((cells * levels - 1,)),
        ],
        compiler_params=pltpu.CompilerParams(
            collective_id=1, has_side_effects=True, vmem_limit_bytes=48 * 1024 * 1024
        ),
        name="climb_and_near",
    )(*inputs)


def local(
    resident_pos, resident_strength, mover_pos, mover_strength, mover_owner, mover_leaf, mover_slot
):
    cells = lax.axis_size("cell")
    cells_x = resident_strength.shape[2]
    place = jnp.stack([lax.axis_index("cell"), lax.axis_index("level")]).astype(jnp.int32)
    movers = [
        mover_pos.reshape(2, -1, LANES),
        mover_strength.reshape(-1, LANES),
        mover_owner.reshape(-1, LANES),
        mover_leaf.reshape(-1, LANES),
        mover_slot.reshape(-1, LANES),
    ]
    own, other, *frames = route(movers, resident_pos, resident_strength)
    got = climb_and_near(own, other, frames)
    owned, got = got[:HALO_LEVELS], got[HALO_LEVELS:]
    return descend(
        place, owned, got[:8], got[8], got[9], own, cells * (cells_x >> HALO_LEVELS)
    )


def solution(mesh):
    return jax.shard_map(
        local,
        mesh=mesh,
        in_specs=(
            P(None, "rep", "level", "cell"),
            P("rep", "level", "cell"),
            P(None, "rep", "level", "cell"),
            P("rep", "level", "cell"),
            P("rep", "level", "cell"),
            P("rep", "level", "cell"),
            P("rep", "level", "cell"),
        ),
        out_specs=P(None, "rep", "level", "cell"),
        check_vma=False,
    )
```

```python
import functools
import math

import jax
import jax.numpy as jnp
import numpy as np
from jax import lax
from jax.experimental import pallas as pl
from jax.experimental.pallas import tpu as pltpu
from jax.sharding import PartitionSpec as P

ORDER = 10
HALO_LEVELS = 4
CAP = 1024
BAND = 8
GROUP = 8
FRONT = 8


precise = lax.Precision.HIGHEST
blob_square = 0.09


def real_form(matrix):
    top_rows = np.concatenate([matrix.real, -matrix.imag], axis=1)
    low_rows = np.concatenate([matrix.imag, matrix.real], axis=1)
    return np.concatenate([top_rows, low_rows], axis=0)


def child_offset(parity_x, parity_y):
    return complex((parity_x - 0.5) / 2.0, (parity_y - 0.5) / 2.0)


def upward_table(parity_x, parity_y):
    offset = child_offset(parity_x, parity_y)
    matrix = np.zeros((ORDER, ORDER), complex)
    for k in range(ORDER):
        for m in range(k + 1):
            matrix[k, m] = math.comb(k, m) * 0.5**m * offset ** (k - m)
    return real_form(matrix)


def downward_table(parity_x, parity_y):
    offset = child_offset(parity_x, parity_y)
    matrix = np.zeros((ORDER, ORDER), complex)
    for m in range(ORDER):
        for l in range(m, ORDER):
            matrix[m, l] = 0.5 ** (m + 1) * math.comb(l, m) * offset ** (l - m)
    return real_form(matrix)


def far_table(step_x, step_y):
    distance = complex(step_x, step_y)
    matrix = np.zeros((ORDER, ORDER), complex)
    for l in range(ORDER):
        for k in range(ORDER):
            matrix[l, k] = (-1) ** (k + 1) * math.comb(k + l, l) * distance ** (-(k + l + 1))
    return real_form(matrix)


CHANNELS = 2 * ORDER
PITCH = 24
HIGH = dict(precision=lax.Precision.HIGHEST, preferred_element_type=jnp.float32)


def pack_starts(cells_y):
    starts = [0]
    for k in range(HALO_LEVELS):
        used = CHANNELS * (cells_y >> k)
        starts.append(starts[-1] + -(-used // 128) * 128)
    return starts


def upward_matrix():
    blocks = [upward_table(px, py) for px in (0, 1) for py in (0, 1)]
    matrix = np.zeros((PITCH, 4 * CHANNELS), np.float32)
    matrix[:CHANNELS] = np.concatenate(blocks, axis=1)
    return matrix


def level_matrix():
    matrix = np.zeros((4 * CHANNELS, 7 * 6 * CHANNELS + 2 * PITCH))
    for px in (0, 1):
        for py in (0, 1):
            rows = slice((2 * px + py) * CHANNELS, (2 * px + py + 1) * CHANNELS)
            for step_x in range(-2 - px, 4 - px):
                for step_y in range(-2 - py, 4 - py):
                    if max(abs(step_x), abs(step_y)) <= 1:
                        continue
                    first = ((step_x + 3) * 6 + step_y + py + 2) * CHANNELS
                    matrix[rows, first : first + CHANNELS] = far_table(step_x, step_y)
            first = 42 * CHANNELS + px * PITCH
            matrix[rows, first : first + CHANNELS] = downward_table(px, py)
    high = np.asarray(matrix, np.float32).astype(jnp.bfloat16)
    low = (matrix - high.astype(np.float64)).astype(np.float32).astype(jnp.bfloat16)
    return np.concatenate([high, low], axis=0)


def top_steps(cells):
    return [d for d in range(1 - cells, cells) if abs(d) >= 2]


def top_matrix(cells):
    steps = top_steps(cells)
    matrix = np.zeros((PITCH, PITCH * len(steps)), np.float32)
    for i, step in enumerate(steps):
        matrix[:CHANNELS, i * PITCH : i * PITCH + CHANNELS] = far_table(step, 0)
    return matrix


def lanes_of(shape):
    return lax.broadcasted_iota(jnp.int32, shape, len(shape) - 1)


def shifted_lanes(value, halo, distance):
    width = value.shape[-1]
    if distance == 0:
        return value
    lane = lanes_of(value.shape)
    if distance > 0:
        return pltpu.roll(jnp.where(lane < distance, halo, value), width - distance, value.ndim - 1)
    return pltpu.roll(jnp.where(lane >= width + distance, halo, value), -distance, value.ndim - 1)


def raise_level(matrix, level_value, cells_y, stride):
    wide = level_value.shape[-1]
    parts = []
    for row in range(cells_y // 2):
        here = level_value[2 * CHANNELS * row : 2 * CHANNELS * (row + 1)]
        parts.append(jnp.concatenate([here, pltpu.roll(here, wide - stride, 1)], axis=0))
    product = jnp.dot(matrix, jnp.concatenate(parts, axis=1), **HIGH)
    return [product[:CHANNELS, wide * row : wide * (row + 1)] for row in range(cells_y // 2)]


def climb_into(own_ref, other_ref, up_ref, zero_ref, one_ref, two_ref, three_ref, four_ref, pack_ref):
    slots, cells_y, cells_x = own_ref.shape[1:]
    levels = [zero_ref, one_ref, two_ref, three_ref]
    for row in range(0, cells_y, BAND):
        here = pl.ds(row, BAND)

        def one_slot(s, sums):
            sums = list(sums)
            for parts_ref in (own_ref, other_ref):
                pos_x, pos_y = parts_ref[0, s, here, :], parts_ref[1, s, here, :]
                real, imag = parts_ref[2, s, here, :], jnp.zeros_like(pos_x)
                for k in range(ORDER):
                    sums[k] = sums[k] + real
                    sums[ORDER + k] = sums[ORDER + k] + imag
                    real, imag = real * pos_x - imag * pos_y, real * pos_y + imag * pos_x
            return tuple(sums)

        zero = jnp.zeros((BAND, cells_x), jnp.float32)
        sums = lax.fori_loop(0, slots, one_slot, (zero,) * CHANNELS)
        for c in range(CHANNELS):
            zero_ref[pl.ds(row * CHANNELS + c, BAND, stride=CHANNELS), :] = sums[c]
    up = up_ref[...]
    pack_ref[...] = jnp.zeros_like(pack_ref)
    starts = pack_starts(cells_y)
    for k in range(HALO_LEVELS):
        count = cells_y >> k
        value = levels[k][...]
        raised = raise_level(up, value, count, 1 << k)
        if k < HALO_LEVELS - 1:
            for row, piece in enumerate(raised):
                levels[k + 1][row * CHANNELS : (row + 1) * CHANNELS, :] = piece
        else:
            lane = lanes_of((cells_x, cells_x))
            source = lax.broadcasted_iota(jnp.int32, (cells_x, cells_x), 0)
            width = cells_x >> HALO_LEVELS
            wanted = (lane - lax.axis_index("cell") * width) * (1 << HALO_LEVELS)
            choose = ((source == wanted) & (wanted >= 0)).astype(jnp.float32)
            four = jnp.concatenate(raised, axis=0)
            four_ref[...] = jnp.dot(four, choose, **HIGH)
        which = lax.broadcasted_iota(jnp.int32, (8, cells_x), 0)
        pick = (lanes_of((8, cells_x)) == edge_lane(which, k, cells_x)).astype(jnp.float32)
        pack_ref[:, starts[k] : starts[k] + count * CHANNELS] = lax.dot_general(
            pick, value, (((1,), (1,)), ((), ())), **HIGH
        )


def edge_lane(which, k, cells_x):
    near = which * (1 << k)
    far = cells_x + (which - 4) * (1 << k)
    return jnp.where(which < 2, near, jnp.where(which < 4, far, -1))


def far_rows(matrix_ref, source_ref, halo_ref, count, stride, parent_ref, out_ref, stage_ref):
    wide = source_ref.shape[-1]
    rows = 6 * CHANNELS
    outer = count // 2
    chunk = min(outer, 4)

    def one_chunk(index, carry):
        for j in range(chunk):
            row = index * chunk + j
            begin = row * 2 * CHANNELS
            if not isinstance(begin, int):
                begin = pl.multiple_of(begin, 8)
            here = pl.ds(begin, rows)
            value = source_ref[here, :]
            halo = 0.0 if halo_ref is None else halo_ref[here, :]
            lanes = slice(j * wide, (j + 1) * wide)
            for step in range(-3, 4):
                first = (step + 3) * rows
                stage_ref[first : first + rows, lanes] = shifted_lanes(value, halo, step * stride)
            above = row * PITCH
            if not isinstance(above, int):
                above = pl.multiple_of(above, 8)
            parent = parent_ref[pl.ds(above, PITCH), :]
            stage_ref[7 * rows : 7 * rows + PITCH, lanes] = parent
            stage_ref[7 * rows + PITCH :, lanes] = pltpu.roll(parent, stride, 1)
        full = stage_ref[:, : chunk * wide]
        high = full.astype(jnp.bfloat16)
        low = (full - high.astype(jnp.float32)).astype(jnp.bfloat16)
        both = jnp.dot(matrix_ref[...], high, preferred_element_type=jnp.float32)
        rest = jnp.dot(matrix_ref[: 4 * CHANNELS, :], low, preferred_element_type=jnp.float32)
        total = both[: 4 * CHANNELS] + (both[4 * CHANNELS :] + rest)
        lane = lanes_of((2 * CHANNELS, wide))
        odd = lax.rem(lane // stride, 2) == 1
        for j in range(chunk):
            lanes = slice(j * wide, (j + 1) * wide)
            chosen = jnp.where(odd, total[2 * CHANNELS :, lanes], total[: 2 * CHANNELS, lanes])
            for py in (0, 1):
                begin = (2 * (index * chunk + j) + py) * PITCH
                if not isinstance(begin, int):
                    begin = pl.multiple_of(begin, 8)
                out_ref[pl.ds(begin, CHANNELS), :] = chosen[py * CHANNELS : (py + 1) * CHANNELS]
        return carry

    if outer == chunk:
        one_chunk(0, 0)
    else:
        lax.fori_loop(0, outer // chunk, one_chunk, 0)


def downward_kernel(
    place_ref, *refs, cells_y, cells_x, coarse_rows, coarse_cells
):
    owned = refs[:HALO_LEVELS]
    before_ref, after_ref, sides = refs[4], refs[5], refs[6:12]
    coarse_ref, matrix_ref, up_ref, top_ref, near_ref, own_ref, out_ref = refs[12:19]
    scratch = list(refs[19:])
    padded, halos, fields = scratch[:4], scratch[4:8], scratch[8:12]
    stage_ref = scratch[12]
    coarse, coarse_fields = scratch[13:17], scratch[17:21]
    entry_ref = scratch[21]
    for ref in fields + coarse + coarse_fields + [entry_ref]:
        ref[...] = jnp.zeros_like(ref)
    edge = 2 * CHANNELS
    total = coarse_ref[0]
    for i in range(1, coarse_ref.shape[0]):
        total = total + coarse_ref[i]
    count = coarse_rows
    level = 0
    up = up_ref[...]
    value = total
    while True:
        coarse[level][edge : edge + count * CHANNELS, :] = value
        if count == 1:
            break
        value = jnp.concatenate(raise_level(up, value, count, 1 << level), axis=0)
        count //= 2
        level += 1
    stride = 1 << level
    steps = top_steps(coarse_cells >> level)
    if steps:
        base = coarse[level][edge : edge + PITCH, :]
        pieces = [shifted_lanes(base, 0.0, d * stride) for d in steps]
        coarse_fields[level][:PITCH, :] = jnp.dot(
            top_ref[...], jnp.concatenate(pieces, axis=0), **HIGH
        )
    while level > 0:
        level -= 1
        count *= 2
        far_rows(
            matrix_ref, coarse[level], None, count, 1 << level,
            coarse_fields[level + 1], coarse_fields[level], stage_ref,
        )
    rows_here = cells_y >> HALO_LEVELS
    width = cells_x >> HALO_LEVELS
    mine = coarse_fields[0][pl.ds(pl.multiple_of(place_ref[1] * rows_here * PITCH, 8), rows_here * PITCH), :]
    lane = lanes_of((cells_x, cells_x))
    source = lax.broadcasted_iota(jnp.int32, (cells_x, cells_x), 0)
    wanted = (source - place_ref[0] * width) * (1 << HALO_LEVELS)
    choose = ((lane == wanted) & (wanted >= 0)).astype(jnp.float32)
    entry_ref[...] = jnp.dot(mine, choose, **HIGH)
    starts = pack_starts(cells_y)
    across = []
    for i in range(3):
        across.append(merged_sides(sides[2 * i], sides[2 * i + 1], 2))
    for k in range(HALO_LEVELS - 1, -1, -1):
        count = cells_y >> k
        used = count * CHANNELS
        padded[k][:edge, :] = before_ref[k * edge : (k + 1) * edge, :]
        padded[k][edge : edge + used, :] = owned[k][...]
        padded[k][edge + used :, :] = after_ref[k * edge : (k + 1) * edge, :]
        which = lax.broadcasted_iota(jnp.int32, (8, cells_x), 0)
        spread = (lanes_of((8, cells_x)) == edge_lane(which, k, cells_x)).astype(jnp.float32)
        begin, end = starts[k], starts[k] + used
        halos[k][:edge, :] = jnp.dot(across[0][end - edge : end], spread, **HIGH)
        halos[k][edge : edge + used, :] = jnp.dot(across[1][begin:end], spread, **HIGH)
        halos[k][edge + used :, :] = jnp.dot(across[2][begin : begin + edge], spread, **HIGH)
        far_rows(
            matrix_ref, padded[k], halos[k], count, 1 << k,
            entry_ref if k == HALO_LEVELS - 1 else fields[k + 1], fields[k], stage_ref,
        )
    half_slots = own_ref.shape[1]
    scale = 1.0 / (2.0 * math.pi)
    for row in range(0, cells_y, BAND):
        here = pl.ds(row, BAND)

        def one_slot(t, carry):
            pos_x, pos_y = own_ref[0, t, here, :], own_ref[1, t, here, :]
            coefs = [
                fields[0][pl.ds(row * PITCH + c, BAND, stride=PITCH), :] for c in range(CHANNELS)
            ]
            real, imag = coefs[ORDER - 1], coefs[2 * ORDER - 1]
            for l in range(ORDER - 2, -1, -1):
                real, imag = (
                    real * pos_x - imag * pos_y + coefs[l],
                    real * pos_y + imag * pos_x + coefs[ORDER + l],
                )
            out_ref[0, t, here, :] = (imag + near_ref[1, t, here, :]) * scale
            out_ref[1, t, here, :] = (real + near_ref[0, t, here, :]) * scale
            return carry

        lax.fori_loop(0, half_slots, one_slot, 0)


VMEM = pl.BlockSpec(memory_space=pltpu.VMEM)
SMEM = pl.BlockSpec(memory_space=pltpu.SMEM)
PARAMS = pltpu.CompilerParams(vmem_limit_bytes=48 * 1024 * 1024)


def descend(place, owned, halo, coarse, near, own, coarse_cells):
    cells_y, cells_x = own.shape[2:]
    coarse_rows = coarse.shape[1] // CHANNELS
    levels = coarse_rows.bit_length()
    top = top_matrix(coarse_cells >> (levels - 1))
    matrix = level_matrix()
    edge = 2 * CHANNELS
    scratch = []
    for extra in range(2):
        for k in range(HALO_LEVELS):
            scratch.append((CHANNELS * (cells_y >> k) + 2 * edge, cells_x))
    for k in range(HALO_LEVELS):
        scratch.append((PITCH * (cells_y >> k), cells_x))
    scratch.append((matrix.shape[1], 4 * cells_x))
    for k in range(levels):
        scratch.append((CHANNELS * (coarse_rows >> k) + 2 * edge, cells_x))
    for k in range(levels):
        scratch.append((PITCH * max(coarse_rows >> k, 1), cells_x))
    scratch.append((PITCH * (cells_y >> HALO_LEVELS), cells_x))
    return pl.pallas_call(
        functools.partial(
            downward_kernel,
            cells_y=cells_y,
            cells_x=cells_x,
            coarse_rows=coarse_rows,
            coarse_cells=coarse_cells,
        ),
        out_shape=jax.ShapeDtypeStruct((2,) + own.shape[1:], jnp.float32),
        in_specs=[SMEM] + [VMEM] * 18,
        out_specs=VMEM,
        scratch_shapes=[pltpu.VMEM(s, jnp.float32) for s in scratch],
        compiler_params=PARAMS,
        name="descend",
    )(
        place, *owned, *halo, coarse, jnp.asarray(matrix),
        jnp.asarray(upward_matrix()), jnp.asarray(top), near, own,
    )


MESH = pl.DeviceIdType.MESH


def position(offset, cells, levels, sign):
    c = lax.axis_index("cell") + sign * offset[0]
    l = lax.axis_index("level") + sign * offset[1]
    r = lax.axis_index("rep")
    r = 1 - r if offset[2] else r
    present = None
    if offset[0] or offset[1]:
        present = (c >= 0) & (c < cells) & (l >= 0) & (l < levels)
    return present, (c, l, r)


def turned(turn, cells, levels, sign):
    return (
        lax.rem(lax.axis_index("cell") + sign * turn[0] + cells, cells),
        lax.rem(lax.axis_index("level") + sign * turn[1] + levels, levels),
        lax.axis_index("rep"),
    )


def guarded(present, action):
    if present is None:
        action()
    else:
        pl.when(present)(action)


def greet(partners):
    barrier = pltpu.get_barrier_semaphore()
    count = jnp.int32(0)
    for present, device in partners:

        def signal(device=device):
            pl.semaphore_signal(barrier, inc=1, device_id=device, device_id_type=MESH)

        guarded(present, signal)
        count = count + (1 if present is None else present.astype(jnp.int32))
    return lambda: pl.semaphore_wait(barrier, count)


class Exchange:
    def __init__(self, sources, outs, offsets, send_sem, recv_sem, cells, levels):
        self.sources, self.outs, self.offsets = sources, outs, offsets
        self.send_sem, self.recv_sem = send_sem, recv_sem
        self.grid = (cells, levels)

    def copy(self, i, device):
        return pltpu.make_async_remote_copy(
            src_ref=self.sources[i],
            dst_ref=self.outs[i],
            send_sem=self.send_sem.at[i],
            recv_sem=self.recv_sem.at[i],
            device_id=device,
            device_id_type=MESH,
        )

    def start(self):
        for i, offset in enumerate(self.offsets):
            present, device = position(offset, *self.grid, -1)
            guarded(present, lambda i=i, device=device: self.copy(i, device).start())

    def wait(self):
        for i, offset in enumerate(self.offsets):
            present, device = position(offset, *self.grid, -1)
            guarded(present, lambda i=i, device=device: self.copy(i, device).wait_send())
            present, device = position(offset, *self.grid, 1)
            guarded(present, lambda i=i, device=device: self.copy(i, device).wait_recv())
            if present is not None:

                @pl.when(jnp.logical_not(present))
                def _(i=i):
                    self.outs[i][...] = jnp.zeros_like(self.outs[i])


AROUND = [(c, l) for l in (-1, 0, 1) for c in (-1, 1)]


LANES = 128
PER_CHUNK = 8
PARTS = 2


def split_parts(value):
    parts = []
    for _ in range(PARTS):
        parts.append(value.astype(jnp.bfloat16).astype(jnp.float32))
        value = value - parts[-1]
    return parts


def joined_parts(acc_ref, v):
    total = acc_ref[:, PARTS * v * LANES : (PARTS * v + 1) * LANES]
    for p in range(PARTS * v + 1, PARTS * (v + 1)):
        total = total + acc_ref[:, p * LANES : (p + 1) * LANES]
    return total


def one_hot_rows(index_row, rows):
    return lax.broadcasted_iota(jnp.int32, (rows, LANES), 0) == index_row


def stage_movers(a_ref, b_ref, j, row, lane, parts):
    lanes = slice(j * LANES, (j + 1) * LANES)
    a_ref[:, lanes] = jnp.where(one_hot_rows(row, a_ref.shape[0]), 1.0, 0.0).astype(jnp.bfloat16)
    at = one_hot_rows(lane, LANES)
    for p, part in enumerate(parts):
        b_ref[p * LANES : (p + 1) * LANES, lanes] = jnp.where(at, part, 0.0).astype(jnp.bfloat16)


def multiply_staged(a_ref, b_ref):
    return lax.dot_general(
        a_ref[...], b_ref[...], (((1,), (1,)), ((), ())), preferred_element_type=jnp.float32
    )


def pack_into(packed_ref, pos_ref, strength_ref, owner_ref, leaf_ref, slot_ref, a_ref, b_ref, acc_ref, leaves):
    cells = packed_ref.shape[0]
    owner = owner_ref[...]
    rows = owner.shape[0]
    first = lax.broadcasted_iota(jnp.int32, (LANES, LANES), 0)
    upto = jnp.where(first <= lanes_of((LANES, LANES)), 1.0, 0.0).astype(jnp.bfloat16)
    ones = jnp.ones((LANES, LANES), jnp.bfloat16)
    before = lax.broadcasted_iota(jnp.int32, (rows, rows), 0) > lanes_of((rows, rows))
    before = jnp.where(before, 1.0, 0.0).astype(jnp.bfloat16)
    dest = jnp.zeros(owner.shape, jnp.float32)
    for o in range(cells):
        mask = jnp.where(owner == o, 1.0, 0.0)
        narrow = mask.astype(jnp.bfloat16)
        inside = jnp.dot(narrow, upto, preferred_element_type=jnp.float32)
        above = jnp.dot(before, narrow, preferred_element_type=jnp.float32).astype(jnp.bfloat16)
        above = jnp.dot(above, ones, preferred_element_type=jnp.float32)
        dest = dest + mask * (inside + above + float(o * CAP - 1))
    dest = dest.astype(jnp.int32)
    address = slot_ref[...] * leaves + leaf_ref[...]
    parts = split_parts(pos_ref[0]) + split_parts(pos_ref[1]) + split_parts(strength_ref[...])
    parts.append(((address >> 8) + 1).astype(jnp.float32))
    parts.append((address & 255).astype(jnp.float32))
    to_row, to_lane = dest >> 7, dest & 127
    for chunk in range(rows // PER_CHUNK):
        for j in range(PER_CHUNK):
            row = slice(chunk * PER_CHUNK + j, chunk * PER_CHUNK + j + 1)
            stage_movers(a_ref, b_ref, j, to_row[row], to_lane[row], [p[row] for p in parts])
        product = multiply_staged(a_ref, b_ref)
        acc_ref[...] = product if chunk == 0 else acc_ref[...] + product
    for v in range(4):
        if v < 3:
            value = joined_parts(acc_ref, v)
        else:
            tail = 3 * PARTS * LANES
            value = (acc_ref[:, tail : tail + LANES] - 1.0) * 256.0 + acc_ref[:, tail + LANES :]
        for c in range(cells):
            packed_ref[c, v * 8 : (v + 1) * 8, :] = value[c * 8 : (c + 1) * 8]


def settle_chunk(arrived, a_ref, b_ref, acc_ref):
    place = arrived[24:32, :].astype(jnp.int32)
    to_row, to_lane = place >> 7, place & 127
    parts = []
    for v in range(3):
        parts += split_parts(arrived[v * 8 : (v + 1) * 8, :])
    parts.append(jnp.ones_like(parts[0]))
    for j in range(PER_CHUNK):
        row = slice(j, j + 1)
        stage_movers(a_ref, b_ref, j, to_row[row], to_lane[row], [p[row] for p in parts])
    acc_ref[...] = acc_ref[...] + multiply_staged(a_ref, b_ref)


def finish_settle(pos_ref, strength_ref, out_ref, first_ref, last_ref, pack_ref, acc_ref):
    half_slots, cells_y, cells_x = strength_ref.shape
    rows = half_slots * cells_y
    taken = acc_ref[:, 3 * PARTS * LANES :] > 0.5
    packed = jnp.zeros(pack_ref.shape, jnp.float32)
    which = lax.broadcasted_iota(jnp.int32, (8, cells_x), 0)
    for v in range(3):
        old = (strength_ref[...] if v == 2 else pos_ref[v]).reshape(rows, cells_x)
        value = jnp.where(taken, joined_parts(acc_ref, v), old)
        out_ref[v] = value.reshape(half_slots, cells_y, cells_x)
        pick = (lanes_of((8, cells_x)) == side_lane(which, v, cells_x)).astype(jnp.float32)
        packed = packed + lax.dot_general(pick, value, (((1,), (1,)), ((), ())), **HIGH)
    pack_ref[...] = packed
    for v in range(3):
        for s in range(half_slots):
            row = v * half_slots + s
            first_ref[row : row + 1, :] = out_ref[v, s, 0:1, :]
            last_ref[row : row + 1, :] = out_ref[v, s, cells_y - 1 :, :]


def particle_offsets():
    offsets = [(0, 0, 1)]
    for rep in (0, 1):
        offsets += [(0, -1, rep), (0, 1, rep)] + [(c, l, rep) for c, l in AROUND]
    return offsets


def side_lane(which, v, cells_x):
    return jnp.where(which == v, 0, jnp.where(which == 4 + v, cells_x - 1, -1))


def merged_sides(left_ref, right_ref, split):
    row = lax.broadcasted_iota(jnp.int32, left_ref.shape, 0)
    return jnp.where(row < split, right_ref[...], left_ref[...]).T


def near_into(out_ref, own_ref, other_ref, frames, src_ref):
    half_slots, cells_y, cells_x = own_ref.shape[1:]
    slot_count = 2 * half_slots
    which = lax.broadcasted_iota(jnp.int32, (8, cells_x), 0)
    for half, ref in enumerate((own_ref, other_ref)):
        before_ref, after_ref, sides = frames[half][0], frames[half][1], frames[half][2:]
        across = [merged_sides(sides[2 * i], sides[2 * i + 1], 4) for i in range(3)]
        for v in range(3):
            pick = (lanes_of((8, cells_x)) == side_lane(which, v, cells_x)).astype(jnp.float32)
            halo = [jnp.dot(a, pick, **HIGH) for a in across]
            halo = [h.reshape(half_slots, cells_y, cells_x) for h in halo]
            rows = slice(v * half_slots, (v + 1) * half_slots)
            top, bottom = before_ref[rows, :], after_ref[rows, :]
            slots = slice(half * half_slots, (half + 1) * half_slots)
            for step in (-1, 0, 1):
                bias = float(step) if v == 0 else 0.0
                src_ref[step + 1, v, slots, FRONT : FRONT + cells_y, :] = (
                    shifted_lanes(ref[v], halo[1], step) + bias
                )
                up = shifted_lanes(top, halo[0][:, cells_y - 1, :], step) + bias
                down = shifted_lanes(bottom, halo[2][:, 0, :], step) + bias
                for s in range(half_slots):
                    slot = half * half_slots + s
                    src_ref[step + 1, v, slot, FRONT - 1 : FRONT, :] = up[s : s + 1]
                    src_ref[step + 1, v, slot, FRONT + cells_y : FRONT + cells_y + 1, :] = down[s : s + 1]

    def one_block(index, carry):
        row = pl.multiple_of((index // (half_slots // GROUP)) * BAND, BAND)
        slot = (index % (half_slots // GROUP)) * GROUP
        here = pl.ds(row, BAND)
        target_x = [own_ref[0, slot + t, here, :] for t in range(GROUP)]
        target_y = [own_ref[1, slot + t, here, :] for t in range(GROUP)]

        def one_source(s, sums):
            sums = list(sums)
            for step_y in (-1, 0, 1):
                there = pl.ds(row + FRONT + step_y, BAND)
                for step_x in (-1, 0, 1):
                    source_x = src_ref[step_x + 1, 0, s, there, :]
                    source_y = src_ref[step_x + 1, 1, s, there, :] + float(step_y)
                    strength = src_ref[step_x + 1, 2, s, there, :]
                    for t in range(0, GROUP, 2):
                        gaps, squares = [], []
                        for u in (t, t + 1):
                            gap_x = target_x[u] - source_x
                            gap_y = target_y[u] - source_y
                            gaps.append((gap_x, gap_y))
                            squares.append(gap_x * gap_x + (gap_y * gap_y + blob_square))
                        shared = strength * pl.reciprocal(squares[0] * squares[1], approx=True)
                        for u, square, (gap_x, gap_y) in zip((t, t + 1), squares[::-1], gaps):
                            weight = shared * square
                            sums[u] = sums[u] + weight * gap_x
                            sums[GROUP + u] = sums[GROUP + u] + weight * gap_y
            return tuple(sums)

        zero = jnp.zeros((BAND, cells_x), jnp.float32)
        sums = lax.fori_loop(0, slot_count, one_source, (zero,) * (2 * GROUP))
        for t in range(GROUP):
            out_ref[0, slot + t, here, :] = sums[t]
            out_ref[1, slot + t, here, :] = -sums[GROUP + t]
        return carry

    lax.fori_loop(0, (cells_y // BAND) * (half_slots // GROUP), one_block, 0)


def near_kernel(*refs, leaves, cells, levels):
    inputs, up_ref, refs = refs[:7], refs[7], refs[8:]
    own_ref, owned, refs = refs[0], refs[1 : 1 + HALO_LEVELS], refs[1 + HALO_LEVELS :]
    received, coarse_ref, near_ref, refs = refs[:8], refs[8], refs[9], refs[10:]
    held, particles, refs = refs[:7], refs[7:24], refs[24:]
    (
        packed_ref, arrived_ref, a_pack, b_pack, acc_pack, a_ref, b_ref, acc_ref,
        first_ref, last_ref, side_ref, load_sem, move_send, move_recv, send_sem, recv_sem,
    ) = refs[:16]
    mine_ref, edges_ref, top_ref, low_ref, src_ref = refs[16:21]
    level_send, level_recv, coarse_send, coarse_recv = refs[21:]
    offsets = particle_offsets()
    turns = [(i, j) for i in range(cells) for j in range(levels) if i or j]
    partners = [(None, turned(turn, cells, levels, 1)) for turn in turns]
    partners += [position(o, cells, levels, 1) for o in offsets if o[2]]
    all_in = greet(partners)
    loads = [
        pltpu.make_async_copy(source, target, load_sem.at[i])
        for i, (source, target) in enumerate(zip(inputs, held))
    ]
    for load in loads:
        load.start()
    for load in loads[:5]:
        load.wait()
    pos_ref, strength_ref = held[5:]
    pack_into(packed_ref, *held[:5], a_pack, b_pack, acc_pack, leaves)
    acc_ref[...] = jnp.zeros_like(acc_ref)
    me = lax.axis_index("cell")
    all_in()

    def move(i):
        target = turned((i, 0), cells, levels, 1)
        return pltpu.make_async_remote_copy(
            src_ref=packed_ref.at[target[0]],
            dst_ref=arrived_ref.at[i],
            send_sem=move_send.at[i],
            recv_sem=move_recv.at[i],
            device_id=target,
            device_id_type=MESH,
        )

    for i in range(1, cells):
        move(i).start()
    arrived_ref[0] = packed_ref[me]
    settle_chunk(arrived_ref[0], a_ref, b_ref, acc_ref)

    def one_source(i, carry):
        move(i).wait_recv()
        settle_chunk(arrived_ref[i], a_ref, b_ref, acc_ref)
        return carry

    lax.fori_loop(1, cells, one_source, 0)
    for load in loads[5:]:
        load.wait()
    finish_settle(pos_ref, strength_ref, own_ref, first_ref, last_ref, side_ref, acc_ref)
    sources = [own_ref] + [last_ref, first_ref] + [side_ref] * 6 + [last_ref, first_ref] + [side_ref] * 6
    swap = Exchange(sources, particles, offsets, send_sem, recv_sem, cells, levels)
    swap.start()
    for i in range(1, cells):
        move(i).wait_send()
    swap.wait()
    climb_into(own_ref, particles[0], up_ref, *owned, mine_ref, edges_ref)
    edge = 2 * CHANNELS
    for k in range(HALO_LEVELS):
        here = slice(k * edge, (k + 1) * edge)
        top_ref[here, :] = owned[k][:edge, :]
        low_ref[here, :] = owned[k][owned[k].shape[0] - edge :, :]
    frames = [particles[1:9], particles[9:17]]
    offsets = [(0, -1, 0), (0, 1, 0)] + [(c, l, 0) for c, l in AROUND]
    sources = [low_ref, top_ref] + [edges_ref] * 6
    swap = Exchange(sources, received, offsets, level_send, level_recv, cells, levels)
    rows = mine_ref.shape[0]

    def copy(i, source, target):
        return pltpu.make_async_remote_copy(
            src_ref=mine_ref,
            dst_ref=coarse_ref.at[source[0], pl.ds(pl.multiple_of(source[1] * rows, 8), rows)],
            send_sem=coarse_send.at[i],
            recv_sem=coarse_recv.at[i],
            device_id=target,
            device_id_type=MESH,
        )

    me = turned((0, 0), cells, levels, 1)
    swap.start()
    for i, turn in enumerate(turns):
        copy(i, me, turned(turn, cells, levels, 1)).start()
    coarse_ref[me[0], pl.ds(pl.multiple_of(me[1] * rows, 8), rows), :] = mine_ref[...]
    near_into(near_ref, own_ref, particles[0], frames, src_ref)
    swap.wait()
    for i, turn in enumerate(turns):
        copy(i, me, turned(turn, cells, levels, 1)).wait_send()
        copy(i, turned(turn, cells, levels, -1), me).wait_recv()


def route_and_near(movers, pos, strength):
    cells, levels = lax.axis_size("cell"), lax.axis_size("level")
    half_slots, cells_y, cells_x = strength.shape
    slot_rows = half_slots * cells_y
    own = (3,) + strength.shape
    edge, side = (3 * half_slots, cells_x), (8, slot_rows)
    particles = [own] + ([edge] * 2 + [side] * 6) * 2
    owned = [(CHANNELS * (cells_y >> k), cells_x) for k in range(HALO_LEVELS)]
    mine = (CHANNELS * (cells_y >> HALO_LEVELS), cells_x)
    edges = (8, pack_starts(cells_y)[-1])
    rows = (2 * CHANNELS * HALO_LEVELS, cells_x)
    shapes = [own] + owned + [rows] * 2 + [edges] * 6
    shapes += [(cells, levels * mine[0], cells_x), (2,) + strength.shape]
    inputs = list(movers) + [pos, strength]
    wide = PER_CHUNK * LANES
    floats = lambda *shape: pltpu.VMEM(shape, jnp.float32)
    halves = lambda *shape: pltpu.VMEM(shape, jnp.bfloat16)
    return pl.pallas_call(
        functools.partial(near_kernel, leaves=cells_y * cells_x, cells=cells, levels=levels),
        out_shape=[jax.ShapeDtypeStruct(s, jnp.float32) for s in shapes],
        in_specs=[pl.BlockSpec(memory_space=pl.ANY)] * len(inputs) + [VMEM],
        out_specs=[VMEM] * len(shapes),
        scratch_shapes=[pltpu.VMEM(x.shape, x.dtype) for x in inputs]
        + [floats(*shape) for shape in particles]
        + [
            floats(cells, 32, LANES),
            floats(cells, 32, LANES),
            halves(cells * 8, wide),
            halves((3 * PARTS + 2) * LANES, wide),
            floats(cells * 8, (3 * PARTS + 2) * LANES),
            halves(slot_rows, wide),
            halves((3 * PARTS + 1) * LANES, wide),
            floats(slot_rows, (3 * PARTS + 1) * LANES),
            floats(*edge),
            floats(*edge),
            floats(*side),
            pltpu.SemaphoreType.DMA((7,)),
            pltpu.SemaphoreType.DMA((cells,)),
            pltpu.SemaphoreType.DMA((cells,)),
            pltpu.SemaphoreType.DMA((17,)),
            pltpu.SemaphoreType.DMA((17,)),
            floats(*mine),
            floats(*edges),
            floats(*rows),
            floats(*rows),
            floats(3, 3, 2 * half_slots, cells_y + 2 * FRONT, cells_x),
            pltpu.SemaphoreType.DMA((8,)),
            pltpu.SemaphoreType.DMA((8,)),
            pltpu.SemaphoreType.DMA((cells * levels - 1,)),
            pltpu.SemaphoreType.DMA((cells * levels - 1,)),
        ],
        compiler_params=pltpu.CompilerParams(
            collective_id=0, has_side_effects=True, vmem_limit_bytes=48 * 1024 * 1024
        ),
        name="route_and_near",
    )(*inputs, jnp.asarray(upward_matrix()))


def local(
    resident_pos, resident_strength, mover_pos, mover_strength, mover_owner, mover_leaf, mover_slot
):
    cells = lax.axis_size("cell")
    cells_x = resident_strength.shape[2]
    place = jnp.stack([lax.axis_index("cell"), lax.axis_index("level")]).astype(jnp.int32)
    movers = [
        mover_pos.reshape(2, -1, LANES),
        mover_strength.reshape(-1, LANES),
        mover_owner.reshape(-1, LANES),
        mover_leaf.reshape(-1, LANES),
        mover_slot.reshape(-1, LANES),
    ]
    own, *got = route_and_near(movers, resident_pos, resident_strength)
    owned, got = got[:HALO_LEVELS], got[HALO_LEVELS:]
    return descend(
        place, owned, got[:8], got[8], got[9], own, cells * (cells_x >> HALO_LEVELS)
    )


def solution(mesh):
    return jax.shard_map(
        local,
        mesh=mesh,
        in_specs=(
            P(None, "rep", "level", "cell"),
            P("rep", "level", "cell"),
            P(None, "rep", "level", "cell"),
            P("rep", "level", "cell"),
            P("rep", "level", "cell"),
            P("rep", "level", "cell"),
            P("rep", "level", "cell"),
        ),
        out_specs=P(None, "rep", "level", "cell"),
        check_vma=False,
    )
```

```python
import functools
import math

import jax
import jax.numpy as jnp
import numpy as np
from jax import lax
from jax.experimental import pallas as pl
from jax.experimental.pallas import tpu as pltpu
from jax.sharding import PartitionSpec as P

ORDER = 10
HALO_LEVELS = 4
CAP = 1024
BAND = 8
GROUP = 8
FRONT = 8


precise = lax.Precision.HIGHEST
blob_square = 0.09


def real_form(matrix):
    top_rows = np.concatenate([matrix.real, -matrix.imag], axis=1)
    low_rows = np.concatenate([matrix.imag, matrix.real], axis=1)
    return np.concatenate([top_rows, low_rows], axis=0)


def child_offset(parity_x, parity_y):
    return complex((parity_x - 0.5) / 2.0, (parity_y - 0.5) / 2.0)


def upward_table(parity_x, parity_y):
    offset = child_offset(parity_x, parity_y)
    matrix = np.zeros((ORDER, ORDER), complex)
    for k in range(ORDER):
        for m in range(k + 1):
            matrix[k, m] = math.comb(k, m) * 0.5**m * offset ** (k - m)
    return real_form(matrix)


def downward_table(parity_x, parity_y):
    offset = child_offset(parity_x, parity_y)
    matrix = np.zeros((ORDER, ORDER), complex)
    for m in range(ORDER):
        for l in range(m, ORDER):
            matrix[m, l] = 0.5 ** (m + 1) * math.comb(l, m) * offset ** (l - m)
    return real_form(matrix)


def far_table(step_x, step_y):
    distance = complex(step_x, step_y)
    matrix = np.zeros((ORDER, ORDER), complex)
    for l in range(ORDER):
        for k in range(ORDER):
            matrix[l, k] = (-1) ** (k + 1) * math.comb(k + l, l) * distance ** (-(k + l + 1))
    return real_form(matrix)


CHANNELS = 2 * ORDER
PITCH = 24
HIGH = dict(precision=lax.Precision.HIGHEST, preferred_element_type=jnp.float32)


def pack_starts(cells_y):
    starts = [0]
    for k in range(HALO_LEVELS):
        used = CHANNELS * (cells_y >> k)
        starts.append(starts[-1] + -(-used // 128) * 128)
    return starts


def upward_matrix():
    blocks = [upward_table(px, py) for px in (0, 1) for py in (0, 1)]
    matrix = np.zeros((PITCH, 4 * CHANNELS), np.float32)
    matrix[:CHANNELS] = np.concatenate(blocks, axis=1)
    return matrix


def level_matrix():
    matrix = np.zeros((4 * CHANNELS, 7 * 6 * CHANNELS + 2 * PITCH))
    for px in (0, 1):
        for py in (0, 1):
            rows = slice((2 * px + py) * CHANNELS, (2 * px + py + 1) * CHANNELS)
            for step_x in range(-2 - px, 4 - px):
                for step_y in range(-2 - py, 4 - py):
                    if max(abs(step_x), abs(step_y)) <= 1:
                        continue
                    first = ((step_x + 3) * 6 + step_y + py + 2) * CHANNELS
                    matrix[rows, first : first + CHANNELS] = far_table(step_x, step_y)
            first = 42 * CHANNELS + px * PITCH
            matrix[rows, first : first + CHANNELS] = downward_table(px, py)
    high = np.asarray(matrix, np.float32).astype(jnp.bfloat16)
    low = (matrix - high.astype(np.float64)).astype(np.float32).astype(jnp.bfloat16)
    return np.concatenate([high, low], axis=0)


def top_steps(cells):
    return [d for d in range(1 - cells, cells) if abs(d) >= 2]


def top_matrix(cells):
    steps = top_steps(cells)
    matrix = np.zeros((PITCH, PITCH * len(steps)), np.float32)
    for i, step in enumerate(steps):
        matrix[:CHANNELS, i * PITCH : i * PITCH + CHANNELS] = far_table(step, 0)
    return matrix


def lanes_of(shape):
    return lax.broadcasted_iota(jnp.int32, shape, len(shape) - 1)


def shifted_lanes(value, halo, distance):
    width = value.shape[-1]
    if distance == 0:
        return value
    lane = lanes_of(value.shape)
    if distance > 0:
        return pltpu.roll(jnp.where(lane < distance, halo, value), width - distance, value.ndim - 1)
    return pltpu.roll(jnp.where(lane >= width + distance, halo, value), -distance, value.ndim - 1)


def raise_level(matrix, level_value, cells_y, stride):
    wide = level_value.shape[-1]
    parts = []
    for row in range(cells_y // 2):
        here = level_value[2 * CHANNELS * row : 2 * CHANNELS * (row + 1)]
        parts.append(jnp.concatenate([here, pltpu.roll(here, wide - stride, 1)], axis=0))
    product = jnp.dot(matrix, jnp.concatenate(parts, axis=1), **HIGH)
    return [product[:CHANNELS, wide * row : wide * (row + 1)] for row in range(cells_y // 2)]


def climb_into(own_ref, other_ref, up_ref, zero_ref, one_ref, two_ref, three_ref, four_ref, pack_ref):
    slots, cells_y, cells_x = own_ref.shape[1:]
    levels = [zero_ref, one_ref, two_ref, three_ref]
    for row in range(0, cells_y, BAND):
        here = pl.ds(row, BAND)

        def one_slot(s, sums):
            sums = list(sums)
            for parts_ref in (own_ref, other_ref):
                pos_x, pos_y = parts_ref[0, s, here, :], parts_ref[1, s, here, :]
                real, imag = parts_ref[2, s, here, :], jnp.zeros_like(pos_x)
                for k in range(ORDER):
                    sums[k] = sums[k] + real
                    sums[ORDER + k] = sums[ORDER + k] + imag
                    real, imag = real * pos_x - imag * pos_y, real * pos_y + imag * pos_x
            return tuple(sums)

        zero = jnp.zeros((BAND, cells_x), jnp.float32)
        sums = lax.fori_loop(0, slots, one_slot, (zero,) * CHANNELS)
        for c in range(CHANNELS):
            zero_ref[pl.ds(row * CHANNELS + c, BAND, stride=CHANNELS), :] = sums[c]
    up = up_ref[...]
    pack_ref[...] = jnp.zeros_like(pack_ref)
    starts = pack_starts(cells_y)
    for k in range(HALO_LEVELS):
        count = cells_y >> k
        value = levels[k][...]
        raised = raise_level(up, value, count, 1 << k)
        if k < HALO_LEVELS - 1:
            for row, piece in enumerate(raised):
                levels[k + 1][row * CHANNELS : (row + 1) * CHANNELS, :] = piece
        else:
            lane = lanes_of((cells_x, cells_x))
            source = lax.broadcasted_iota(jnp.int32, (cells_x, cells_x), 0)
            width = cells_x >> HALO_LEVELS
            wanted = (lane - lax.axis_index("cell") * width) * (1 << HALO_LEVELS)
            choose = ((source == wanted) & (wanted >= 0)).astype(jnp.float32)
            four = jnp.concatenate(raised, axis=0)
            four_ref[...] = jnp.dot(four, choose, **HIGH)
        which = lax.broadcasted_iota(jnp.int32, (8, cells_x), 0)
        pick = (lanes_of((8, cells_x)) == edge_lane(which, k, cells_x)).astype(jnp.float32)
        pack_ref[:, starts[k] : starts[k] + count * CHANNELS] = lax.dot_general(
            pick, value, (((1,), (1,)), ((), ())), **HIGH
        )


def edge_lane(which, k, cells_x):
    near = which * (1 << k)
    far = cells_x + (which - 4) * (1 << k)
    return jnp.where(which < 2, near, jnp.where(which < 4, far, -1))


def far_rows(matrix_ref, source_ref, halo_ref, count, stride, parent_ref, out_ref, stage_ref):
    wide = source_ref.shape[-1]
    rows = 6 * CHANNELS
    outer = count // 2
    chunk = min(outer, 4)

    def one_chunk(index, carry):
        for j in range(chunk):
            row = index * chunk + j
            begin = row * 2 * CHANNELS
            if not isinstance(begin, int):
                begin = pl.multiple_of(begin, 8)
            here = pl.ds(begin, rows)
            value = source_ref[here, :]
            halo = 0.0 if halo_ref is None else halo_ref[here, :]
            lanes = slice(j * wide, (j + 1) * wide)
            for step in range(-3, 4):
                first = (step + 3) * rows
                stage_ref[first : first + rows, lanes] = shifted_lanes(value, halo, step * stride)
            above = row * PITCH
            if not isinstance(above, int):
                above = pl.multiple_of(above, 8)
            parent = parent_ref[pl.ds(above, PITCH), :]
            stage_ref[7 * rows : 7 * rows + PITCH, lanes] = parent
            stage_ref[7 * rows + PITCH :, lanes] = pltpu.roll(parent, stride, 1)
        full = stage_ref[:, : chunk * wide]
        high = full.astype(jnp.bfloat16)
        low = (full - high.astype(jnp.float32)).astype(jnp.bfloat16)
        both = jnp.dot(matrix_ref[...], high, preferred_element_type=jnp.float32)
        rest = jnp.dot(matrix_ref[: 4 * CHANNELS, :], low, preferred_element_type=jnp.float32)
        total = both[: 4 * CHANNELS] + (both[4 * CHANNELS :] + rest)
        lane = lanes_of((2 * CHANNELS, wide))
        odd = lax.rem(lane // stride, 2) == 1
        for j in range(chunk):
            lanes = slice(j * wide, (j + 1) * wide)
            chosen = jnp.where(odd, total[2 * CHANNELS :, lanes], total[: 2 * CHANNELS, lanes])
            for py in (0, 1):
                begin = (2 * (index * chunk + j) + py) * PITCH
                if not isinstance(begin, int):
                    begin = pl.multiple_of(begin, 8)
                out_ref[pl.ds(begin, CHANNELS), :] = chosen[py * CHANNELS : (py + 1) * CHANNELS]
        return carry

    if outer == chunk:
        one_chunk(0, 0)
    else:
        lax.fori_loop(0, outer // chunk, one_chunk, 0)


def downward_kernel(
    place_ref, *refs, cells_y, cells_x, coarse_rows, coarse_cells
):
    owned = refs[:HALO_LEVELS]
    before_ref, after_ref, sides = refs[4], refs[5], refs[6:12]
    coarse_ref, matrix_ref, up_ref, top_ref, near_ref, own_ref, out_ref = refs[12:19]
    scratch = list(refs[19:])
    padded, halos, fields = scratch[:4], scratch[4:8], scratch[8:12]
    stage_ref = scratch[12]
    coarse, coarse_fields = scratch[13:17], scratch[17:21]
    entry_ref = scratch[21]
    for ref in fields + coarse + coarse_fields + [entry_ref]:
        ref[...] = jnp.zeros_like(ref)
    edge = 2 * CHANNELS
    total = coarse_ref[0]
    for i in range(1, coarse_ref.shape[0]):
        total = total + coarse_ref[i]
    count = coarse_rows
    level = 0
    up = up_ref[...]
    value = total
    while True:
        coarse[level][edge : edge + count * CHANNELS, :] = value
        if count == 1:
            break
        value = jnp.concatenate(raise_level(up, value, count, 1 << level), axis=0)
        count //= 2
        level += 1
    stride = 1 << level
    steps = top_steps(coarse_cells >> level)
    if steps:
        base = coarse[level][edge : edge + PITCH, :]
        pieces = [shifted_lanes(base, 0.0, d * stride) for d in steps]
        coarse_fields[level][:PITCH, :] = jnp.dot(
            top_ref[...], jnp.concatenate(pieces, axis=0), **HIGH
        )
    while level > 0:
        level -= 1
        count *= 2
        far_rows(
            matrix_ref, coarse[level], None, count, 1 << level,
            coarse_fields[level + 1], coarse_fields[level], stage_ref,
        )
    rows_here = cells_y >> HALO_LEVELS
    width = cells_x >> HALO_LEVELS
    mine = coarse_fields[0][pl.ds(pl.multiple_of(place_ref[1] * rows_here * PITCH, 8), rows_here * PITCH), :]
    lane = lanes_of((cells_x, cells_x))
    source = lax.broadcasted_iota(jnp.int32, (cells_x, cells_x), 0)
    wanted = (source - place_ref[0] * width) * (1 << HALO_LEVELS)
    choose = ((lane == wanted) & (wanted >= 0)).astype(jnp.float32)
    entry_ref[...] = jnp.dot(mine, choose, **HIGH)
    starts = pack_starts(cells_y)
    across = []
    for i in range(3):
        across.append(merged_sides(sides[2 * i], sides[2 * i + 1], 2))
    for k in range(HALO_LEVELS - 1, -1, -1):
        count = cells_y >> k
        used = count * CHANNELS
        padded[k][:edge, :] = before_ref[k * edge : (k + 1) * edge, :]
        padded[k][edge : edge + used, :] = owned[k][...]
        padded[k][edge + used :, :] = after_ref[k * edge : (k + 1) * edge, :]
        which = lax.broadcasted_iota(jnp.int32, (8, cells_x), 0)
        spread = (lanes_of((8, cells_x)) == edge_lane(which, k, cells_x)).astype(jnp.float32)
        begin, end = starts[k], starts[k] + used
        halos[k][:edge, :] = jnp.dot(across[0][end - edge : end], spread, **HIGH)
        halos[k][edge : edge + used, :] = jnp.dot(across[1][begin:end], spread, **HIGH)
        halos[k][edge + used :, :] = jnp.dot(across[2][begin : begin + edge], spread, **HIGH)
        far_rows(
            matrix_ref, padded[k], halos[k], count, 1 << k,
            entry_ref if k == HALO_LEVELS - 1 else fields[k + 1], fields[k], stage_ref,
        )
    half_slots = own_ref.shape[1]
    scale = 1.0 / (2.0 * math.pi)
    for row in range(0, cells_y, BAND):
        here = pl.ds(row, BAND)

        def one_slot(t, carry):
            pos_x, pos_y = own_ref[0, t, here, :], own_ref[1, t, here, :]
            coefs = [
                fields[0][pl.ds(row * PITCH + c, BAND, stride=PITCH), :] for c in range(CHANNELS)
            ]
            real, imag = coefs[ORDER - 1], coefs[2 * ORDER - 1]
            for l in range(ORDER - 2, -1, -1):
                real, imag = (
                    real * pos_x - imag * pos_y + coefs[l],
                    real * pos_y + imag * pos_x + coefs[ORDER + l],
                )
            out_ref[0, t, here, :] = (imag + near_ref[1, t, here, :]) * scale
            out_ref[1, t, here, :] = (real + near_ref[0, t, here, :]) * scale
            return carry

        lax.fori_loop(0, half_slots, one_slot, 0)


VMEM = pl.BlockSpec(memory_space=pltpu.VMEM)
SMEM = pl.BlockSpec(memory_space=pltpu.SMEM)
PARAMS = pltpu.CompilerParams(vmem_limit_bytes=48 * 1024 * 1024)


def descend(place, owned, halo, coarse, near, own, coarse_cells):
    cells_y, cells_x = own.shape[2:]
    coarse_rows = coarse.shape[1] // CHANNELS
    levels = coarse_rows.bit_length()
    top = top_matrix(coarse_cells >> (levels - 1))
    matrix = level_matrix()
    edge = 2 * CHANNELS
    scratch = []
    for extra in range(2):
        for k in range(HALO_LEVELS):
            scratch.append((CHANNELS * (cells_y >> k) + 2 * edge, cells_x))
    for k in range(HALO_LEVELS):
        scratch.append((PITCH * (cells_y >> k), cells_x))
    scratch.append((matrix.shape[1], 4 * cells_x))
    for k in range(levels):
        scratch.append((CHANNELS * (coarse_rows >> k) + 2 * edge, cells_x))
    for k in range(levels):
        scratch.append((PITCH * max(coarse_rows >> k, 1), cells_x))
    scratch.append((PITCH * (cells_y >> HALO_LEVELS), cells_x))
    return pl.pallas_call(
        functools.partial(
            downward_kernel,
            cells_y=cells_y,
            cells_x=cells_x,
            coarse_rows=coarse_rows,
            coarse_cells=coarse_cells,
        ),
        out_shape=jax.ShapeDtypeStruct((2,) + own.shape[1:], jnp.float32),
        in_specs=[SMEM] + [VMEM] * 18,
        out_specs=VMEM,
        scratch_shapes=[pltpu.VMEM(s, jnp.float32) for s in scratch],
        compiler_params=PARAMS,
        name="descend",
    )(
        place, *owned, *halo, coarse, jnp.asarray(matrix),
        jnp.asarray(upward_matrix()), jnp.asarray(top), near, own,
    )


MESH = pl.DeviceIdType.MESH


def position(offset, cells, levels, sign):
    c = lax.axis_index("cell") + sign * offset[0]
    l = lax.axis_index("level") + sign * offset[1]
    r = lax.axis_index("rep")
    r = 1 - r if offset[2] else r
    present = None
    if offset[0] or offset[1]:
        present = (c >= 0) & (c < cells) & (l >= 0) & (l < levels)
    return present, (c, l, r)


def turned(turn, cells, levels, sign):
    return (
        lax.rem(lax.axis_index("cell") + sign * turn[0] + cells, cells),
        lax.rem(lax.axis_index("level") + sign * turn[1] + levels, levels),
        lax.axis_index("rep"),
    )


def guarded(present, action):
    if present is None:
        action()
    else:
        pl.when(present)(action)


def greet(partners):
    barrier = pltpu.get_barrier_semaphore()
    count = jnp.int32(0)
    for present, device in partners:

        def signal(device=device):
            pl.semaphore_signal(barrier, inc=1, device_id=device, device_id_type=MESH)

        guarded(present, signal)
        count = count + (1 if present is None else present.astype(jnp.int32))
    return lambda: pl.semaphore_wait(barrier, count)


class Exchange:
    def __init__(self, sources, outs, offsets, send_sem, recv_sem, cells, levels):
        self.sources, self.outs, self.offsets = sources, outs, offsets
        self.send_sem, self.recv_sem = send_sem, recv_sem
        self.grid = (cells, levels)

    def copy(self, i, device):
        return pltpu.make_async_remote_copy(
            src_ref=self.sources[i],
            dst_ref=self.outs[i],
            send_sem=self.send_sem.at[i],
            recv_sem=self.recv_sem.at[i],
            device_id=device,
            device_id_type=MESH,
        )

    def start(self):
        for i, offset in enumerate(self.offsets):
            present, device = position(offset, *self.grid, -1)
            guarded(present, lambda i=i, device=device: self.copy(i, device).start())

    def wait(self):
        for i, offset in enumerate(self.offsets):
            present, device = position(offset, *self.grid, -1)
            guarded(present, lambda i=i, device=device: self.copy(i, device).wait_send())
            present, device = position(offset, *self.grid, 1)
            guarded(present, lambda i=i, device=device: self.copy(i, device).wait_recv())
            if present is not None:

                @pl.when(jnp.logical_not(present))
                def _(i=i):
                    self.outs[i][...] = jnp.zeros_like(self.outs[i])


AROUND = [(c, l) for l in (-1, 0, 1) for c in (-1, 1)]


LANES = 128
PER_CHUNK = 8
PARTS = 2


def split_parts(value):
    parts = []
    for _ in range(PARTS):
        parts.append(value.astype(jnp.bfloat16).astype(jnp.float32))
        value = value - parts[-1]
    return parts


def joined_parts(acc_ref, v):
    total = acc_ref[:, PARTS * v * LANES : (PARTS * v + 1) * LANES]
    for p in range(PARTS * v + 1, PARTS * (v + 1)):
        total = total + acc_ref[:, p * LANES : (p + 1) * LANES]
    return total


def one_hot_rows(index_row, rows):
    return lax.broadcasted_iota(jnp.int32, (rows, LANES), 0) == index_row


def stage_movers(a_ref, b_ref, j, row, lane, parts):
    lanes = slice(j * LANES, (j + 1) * LANES)
    a_ref[:, lanes] = jnp.where(one_hot_rows(row, a_ref.shape[0]), 1.0, 0.0).astype(jnp.bfloat16)
    at = one_hot_rows(lane, LANES)
    for p, part in enumerate(parts):
        b_ref[p * LANES : (p + 1) * LANES, lanes] = jnp.where(at, part, 0.0).astype(jnp.bfloat16)


def multiply_staged(a_ref, b_ref):
    return lax.dot_general(
        a_ref[...], b_ref[...], (((1,), (1,)), ((), ())), preferred_element_type=jnp.float32
    )


def pack_into(packed_ref, pos_ref, strength_ref, owner_ref, leaf_ref, slot_ref, a_ref, b_ref, acc_ref, leaves):
    cells = packed_ref.shape[0]
    owner = owner_ref[...]
    rows = owner.shape[0]
    first = lax.broadcasted_iota(jnp.int32, (LANES, LANES), 0)
    upto = jnp.where(first <= lanes_of((LANES, LANES)), 1.0, 0.0).astype(jnp.bfloat16)
    ones = jnp.ones((LANES, LANES), jnp.bfloat16)
    before = lax.broadcasted_iota(jnp.int32, (rows, rows), 0) > lanes_of((rows, rows))
    before = jnp.where(before, 1.0, 0.0).astype(jnp.bfloat16)
    dest = jnp.zeros(owner.shape, jnp.float32)
    for o in range(cells):
        mask = jnp.where(owner == o, 1.0, 0.0)
        narrow = mask.astype(jnp.bfloat16)
        inside = jnp.dot(narrow, upto, preferred_element_type=jnp.float32)
        above = jnp.dot(before, narrow, preferred_element_type=jnp.float32).astype(jnp.bfloat16)
        above = jnp.dot(above, ones, preferred_element_type=jnp.float32)
        dest = dest + mask * (inside + above + float(o * CAP - 1))
    dest = dest.astype(jnp.int32)
    address = slot_ref[...] * leaves + leaf_ref[...]
    parts = split_parts(pos_ref[0]) + split_parts(pos_ref[1]) + split_parts(strength_ref[...])
    parts.append(((address >> 8) + 1).astype(jnp.float32))
    parts.append((address & 255).astype(jnp.float32))
    to_row, to_lane = dest >> 7, dest & 127
    for chunk in range(rows // PER_CHUNK):
        for j in range(PER_CHUNK):
            row = slice(chunk * PER_CHUNK + j, chunk * PER_CHUNK + j + 1)
            stage_movers(a_ref, b_ref, j, to_row[row], to_lane[row], [p[row] for p in parts])
        product = multiply_staged(a_ref, b_ref)
        acc_ref[...] = product if chunk == 0 else acc_ref[...] + product
    for v in range(4):
        if v < 3:
            value = joined_parts(acc_ref, v)
        else:
            tail = 3 * PARTS * LANES
            value = (acc_ref[:, tail : tail + LANES] - 1.0) * 256.0 + acc_ref[:, tail + LANES :]
        for c in range(cells):
            packed_ref[c, v * 8 : (v + 1) * 8, :] = value[c * 8 : (c + 1) * 8]


def settle_chunk(arrived, a_ref, b_ref, acc_ref):
    place = arrived[24:32, :].astype(jnp.int32)
    to_row, to_lane = place >> 7, place & 127
    parts = []
    for v in range(3):
        parts += split_parts(arrived[v * 8 : (v + 1) * 8, :])
    parts.append(jnp.ones_like(parts[0]))
    for j in range(PER_CHUNK):
        row = slice(j, j + 1)
        stage_movers(a_ref, b_ref, j, to_row[row], to_lane[row], [p[row] for p in parts])
    acc_ref[...] = acc_ref[...] + multiply_staged(a_ref, b_ref)


def finish_settle(pos_ref, strength_ref, out_ref, first_ref, last_ref, pack_ref, acc_ref):
    half_slots, cells_y, cells_x = strength_ref.shape
    rows = half_slots * cells_y
    taken = acc_ref[:, 3 * PARTS * LANES :] > 0.5
    packed = jnp.zeros(pack_ref.shape, jnp.float32)
    which = lax.broadcasted_iota(jnp.int32, (8, cells_x), 0)
    for v in range(3):
        old = (strength_ref[...] if v == 2 else pos_ref[v]).reshape(rows, cells_x)
        value = jnp.where(taken, joined_parts(acc_ref, v), old)
        out_ref[v] = value.reshape(half_slots, cells_y, cells_x)
        pick = (lanes_of((8, cells_x)) == side_lane(which, v, cells_x)).astype(jnp.float32)
        packed = packed + lax.dot_general(pick, value, (((1,), (1,)), ((), ())), **HIGH)
    pack_ref[...] = packed
    for v in range(3):
        for s in range(half_slots):
            row = v * half_slots + s
            first_ref[row : row + 1, :] = out_ref[v, s, 0:1, :]
            last_ref[row : row + 1, :] = out_ref[v, s, cells_y - 1 :, :]


def particle_offsets():
    offsets = [(0, 0, 1)]
    for rep in (0, 1):
        offsets += [(0, -1, rep), (0, 1, rep)] + [(c, l, rep) for c, l in AROUND]
    return offsets


def side_lane(which, v, cells_x):
    return jnp.where(which == v, 0, jnp.where(which == 4 + v, cells_x - 1, -1))


def merged_sides(left_ref, right_ref, split):
    row = lax.broadcasted_iota(jnp.int32, left_ref.shape, 0)
    return jnp.where(row < split, right_ref[...], left_ref[...]).T


def near_into(out_ref, own_ref, other_ref, frames, src_ref):
    half_slots, cells_y, cells_x = own_ref.shape[1:]
    slot_count = 2 * half_slots
    which = lax.broadcasted_iota(jnp.int32, (8, cells_x), 0)
    for half, ref in enumerate((own_ref, other_ref)):
        before_ref, after_ref, sides = frames[half][0], frames[half][1], frames[half][2:]
        across = [merged_sides(sides[2 * i], sides[2 * i + 1], 4) for i in range(3)]
        for v in range(3):
            pick = (lanes_of((8, cells_x)) == side_lane(which, v, cells_x)).astype(jnp.float32)
            halo = [jnp.dot(a, pick, **HIGH) for a in across]
            halo = [h.reshape(half_slots, cells_y, cells_x) for h in halo]
            rows = slice(v * half_slots, (v + 1) * half_slots)
            top, bottom = before_ref[rows, :], after_ref[rows, :]
            slots = slice(half * half_slots, (half + 1) * half_slots)
            for step in (-1, 0, 1):
                bias = float(step) if v == 0 else 0.0
                src_ref[step + 1, v, slots, FRONT : FRONT + cells_y, :] = (
                    shifted_lanes(ref[v], halo[1], step) + bias
                )
                up = shifted_lanes(top, halo[0][:, cells_y - 1, :], step) + bias
                down = shifted_lanes(bottom, halo[2][:, 0, :], step) + bias
                for s in range(half_slots):
                    slot = half * half_slots + s
                    src_ref[step + 1, v, slot, FRONT - 1 : FRONT, :] = up[s : s + 1]
                    src_ref[step + 1, v, slot, FRONT + cells_y : FRONT + cells_y + 1, :] = down[s : s + 1]

    def one_block(index, carry):
        row = pl.multiple_of((index // (half_slots // GROUP)) * BAND, BAND)
        slot = (index % (half_slots // GROUP)) * GROUP
        here = pl.ds(row, BAND)
        target_x = [own_ref[0, slot + t, here, :] for t in range(GROUP)]
        target_y = [own_ref[1, slot + t, here, :] for t in range(GROUP)]

        def one_source(s, sums):
            sums = list(sums)
            for step_y in (-1, 0, 1):
                there = pl.ds(row + FRONT + step_y, BAND)
                for step_x in (-1, 0, 1):
                    source_x = src_ref[step_x + 1, 0, s, there, :]
                    source_y = src_ref[step_x + 1, 1, s, there, :] + float(step_y)
                    strength = src_ref[step_x + 1, 2, s, there, :]
                    for t in range(GROUP):
                        gap_x = target_x[t] - source_x
                        gap_y = target_y[t] - source_y
                        square = gap_x * gap_x + (gap_y * gap_y + blob_square)
                        weight = strength * pl.reciprocal(square, approx=True)
                        sums[t] = sums[t] + weight * gap_x
                        sums[GROUP + t] = sums[GROUP + t] + weight * gap_y
            return tuple(sums)

        zero = jnp.zeros((BAND, cells_x), jnp.float32)
        sums = lax.fori_loop(0, slot_count, one_source, (zero,) * (2 * GROUP))
        for t in range(GROUP):
            out_ref[0, slot + t, here, :] = sums[t]
            out_ref[1, slot + t, here, :] = -sums[GROUP + t]
        return carry

    lax.fori_loop(0, (cells_y // BAND) * (half_slots // GROUP), one_block, 0)


def near_kernel(*refs, leaves, cells, levels):
    inputs, up_ref, refs = refs[:7], refs[7], refs[8:]
    own_ref, owned, refs = refs[0], refs[1 : 1 + HALO_LEVELS], refs[1 + HALO_LEVELS :]
    received, coarse_ref, near_ref, refs = refs[:8], refs[8], refs[9], refs[10:]
    held, particles, refs = refs[:7], refs[7:24], refs[24:]
    (
        packed_ref, arrived_ref, a_pack, b_pack, acc_pack, a_ref, b_ref, acc_ref,
        first_ref, last_ref, side_ref, load_sem, move_send, move_recv, send_sem, recv_sem,
    ) = refs[:16]
    mine_ref, edges_ref, top_ref, low_ref, src_ref = refs[16:21]
    level_send, level_recv, coarse_send, coarse_recv = refs[21:]
    offsets = particle_offsets()
    turns = [(i, j) for i in range(cells) for j in range(levels) if i or j]
    partners = [(None, turned(turn, cells, levels, 1)) for turn in turns]
    partners += [position(o, cells, levels, 1) for o in offsets if o[2]]
    all_in = greet(partners)
    loads = [
        pltpu.make_async_copy(source, target, load_sem.at[i])
        for i, (source, target) in enumerate(zip(inputs, held))
    ]
    for load in loads:
        load.start()
    for load in loads[:5]:
        load.wait()
    pos_ref, strength_ref = held[5:]
    pack_into(packed_ref, *held[:5], a_pack, b_pack, acc_pack, leaves)
    acc_ref[...] = jnp.zeros_like(acc_ref)
    me = lax.axis_index("cell")
    all_in()

    def move(i):
        target = turned((i, 0), cells, levels, 1)
        return pltpu.make_async_remote_copy(
            src_ref=packed_ref.at[target[0]],
            dst_ref=arrived_ref.at[i],
            send_sem=move_send.at[i],
            recv_sem=move_recv.at[i],
            device_id=target,
            device_id_type=MESH,
        )

    for i in range(1, cells):
        move(i).start()
    arrived_ref[0] = packed_ref[me]
    settle_chunk(arrived_ref[0], a_ref, b_ref, acc_ref)

    def one_source(i, carry):
        move(i).wait_recv()
        settle_chunk(arrived_ref[i], a_ref, b_ref, acc_ref)
        return carry

    lax.fori_loop(1, cells, one_source, 0)
    for load in loads[5:]:
        load.wait()
    finish_settle(pos_ref, strength_ref, own_ref, first_ref, last_ref, side_ref, acc_ref)
    sources = [own_ref] + [last_ref, first_ref] + [side_ref] * 6 + [last_ref, first_ref] + [side_ref] * 6
    swap = Exchange(sources, particles, offsets, send_sem, recv_sem, cells, levels)
    swap.start()
    for i in range(1, cells):
        move(i).wait_send()
    swap.wait()
    climb_into(own_ref, particles[0], up_ref, *owned, mine_ref, edges_ref)
    edge = 2 * CHANNELS
    for k in range(HALO_LEVELS):
        here = slice(k * edge, (k + 1) * edge)
        top_ref[here, :] = owned[k][:edge, :]
        low_ref[here, :] = owned[k][owned[k].shape[0] - edge :, :]
    frames = [particles[1:9], particles[9:17]]
    offsets = [(0, -1, 0), (0, 1, 0)] + [(c, l, 0) for c, l in AROUND]
    sources = [low_ref, top_ref] + [edges_ref] * 6
    swap = Exchange(sources, received, offsets, level_send, level_recv, cells, levels)
    rows = mine_ref.shape[0]

    def copy(i, source, target):
        return pltpu.make_async_remote_copy(
            src_ref=mine_ref,
            dst_ref=coarse_ref.at[source[0], pl.ds(pl.multiple_of(source[1] * rows, 8), rows)],
            send_sem=coarse_send.at[i],
            recv_sem=coarse_recv.at[i],
            device_id=target,
            device_id_type=MESH,
        )

    me = turned((0, 0), cells, levels, 1)
    swap.start()
    for i, turn in enumerate(turns):
        copy(i, me, turned(turn, cells, levels, 1)).start()
    coarse_ref[me[0], pl.ds(pl.multiple_of(me[1] * rows, 8), rows), :] = mine_ref[...]
    near_into(near_ref, own_ref, particles[0], frames, src_ref)
    swap.wait()
    for i, turn in enumerate(turns):
        copy(i, me, turned(turn, cells, levels, 1)).wait_send()
        copy(i, turned(turn, cells, levels, -1), me).wait_recv()


def route_and_near(movers, pos, strength):
    cells, levels = lax.axis_size("cell"), lax.axis_size("level")
    half_slots, cells_y, cells_x = strength.shape
    slot_rows = half_slots * cells_y
    own = (3,) + strength.shape
    edge, side = (3 * half_slots, cells_x), (8, slot_rows)
    particles = [own] + ([edge] * 2 + [side] * 6) * 2
    owned = [(CHANNELS * (cells_y >> k), cells_x) for k in range(HALO_LEVELS)]
    mine = (CHANNELS * (cells_y >> HALO_LEVELS), cells_x)
    edges = (8, pack_starts(cells_y)[-1])
    rows = (2 * CHANNELS * HALO_LEVELS, cells_x)
    shapes = [own] + owned + [rows] * 2 + [edges] * 6
    shapes += [(cells, levels * mine[0], cells_x), (2,) + strength.shape]
    inputs = list(movers) + [pos, strength]
    wide = PER_CHUNK * LANES
    floats = lambda *shape: pltpu.VMEM(shape, jnp.float32)
    halves = lambda *shape: pltpu.VMEM(shape, jnp.bfloat16)
    return pl.pallas_call(
        functools.partial(near_kernel, leaves=cells_y * cells_x, cells=cells, levels=levels),
        out_shape=[jax.ShapeDtypeStruct(s, jnp.float32) for s in shapes],
        in_specs=[pl.BlockSpec(memory_space=pl.ANY)] * len(inputs) + [VMEM],
        out_specs=[VMEM] * len(shapes),
        scratch_shapes=[pltpu.VMEM(x.shape, x.dtype) for x in inputs]
        + [floats(*shape) for shape in particles]
        + [
            floats(cells, 32, LANES),
            floats(cells, 32, LANES),
            halves(cells * 8, wide),
            halves((3 * PARTS + 2) * LANES, wide),
            floats(cells * 8, (3 * PARTS + 2) * LANES),
            halves(slot_rows, wide),
            halves((3 * PARTS + 1) * LANES, wide),
            floats(slot_rows, (3 * PARTS + 1) * LANES),
            floats(*edge),
            floats(*edge),
            floats(*side),
            pltpu.SemaphoreType.DMA((7,)),
            pltpu.SemaphoreType.DMA((cells,)),
            pltpu.SemaphoreType.DMA((cells,)),
            pltpu.SemaphoreType.DMA((17,)),
            pltpu.SemaphoreType.DMA((17,)),
            floats(*mine),
            floats(*edges),
            floats(*rows),
            floats(*rows),
            floats(3, 3, 2 * half_slots, cells_y + 2 * FRONT, cells_x),
            pltpu.SemaphoreType.DMA((8,)),
            pltpu.SemaphoreType.DMA((8,)),
            pltpu.SemaphoreType.DMA((cells * levels - 1,)),
            pltpu.SemaphoreType.DMA((cells * levels - 1,)),
        ],
        compiler_params=pltpu.CompilerParams(
            collective_id=0, has_side_effects=True, vmem_limit_bytes=48 * 1024 * 1024
        ),
        name="route_and_near",
    )(*inputs, jnp.asarray(upward_matrix()))


def local(
    resident_pos, resident_strength, mover_pos, mover_strength, mover_owner, mover_leaf, mover_slot
):
    cells = lax.axis_size("cell")
    cells_x = resident_strength.shape[2]
    place = jnp.stack([lax.axis_index("cell"), lax.axis_index("level")]).astype(jnp.int32)
    movers = [
        mover_pos.reshape(2, -1, LANES),
        mover_strength.reshape(-1, LANES),
        mover_owner.reshape(-1, LANES),
        mover_leaf.reshape(-1, LANES),
        mover_slot.reshape(-1, LANES),
    ]
    own, *got = route_and_near(movers, resident_pos, resident_strength)
    owned, got = got[:HALO_LEVELS], got[HALO_LEVELS:]
    return descend(
        place, owned, got[:8], got[8], got[9], own, cells * (cells_x >> HALO_LEVELS)
    )


def solution(mesh):
    return jax.shard_map(
        local,
        mesh=mesh,
        in_specs=(
            P(None, "rep", "level", "cell"),
            P("rep", "level", "cell"),
            P(None, "rep", "level", "cell"),
            P("rep", "level", "cell"),
            P("rep", "level", "cell"),
            P("rep", "level", "cell"),
            P("rep", "level", "cell"),
        ),
        out_specs=P(None, "rep", "level", "cell"),
        check_vma=False,
    )
```
